32 devices in a mesh: ra: 8 (over z, core), dec: 2 (over y), freq: 2 (over x).
Axes of the slice: x: 2, y: 2, z: 4, core: 2. Of those that a mesh axis runs over, the one named last changes fastest.
Arguments:
- tokens: bfloat16 [64, 32, 64, 192], P('ra', 'dec', 'freq'), may hold values from -12 to 12
- attn_gain: float32 [2, 192], replicated, may hold values from 0.1 to 1.9
- qkv_weight: bfloat16 [2, 192, 576], replicated, may hold values from -3 to 3
- out_weight: bfloat16 [2, 192, 192], replicated, may hold values from -0.4375 to 0.4375
- mlp_gain: float32 [2, 192], replicated, may hold values from 0.1 to 1.9
- up_weight: bfloat16 [2, 192, 768], replicated, may hold values from -0.4375 to 0.4375
- down_weight: bfloat16 [2, 768, 192], replicated, may hold values from -0.21875 to 0.21875
- merge_gain: float32 [1536], replicated, may hold values from 0.1 to 1.9
- merge_weight: bfloat16 [1536, 384], replicated, may hold values from -0.15625 to 0.15625
Outputs:
- merged: bfloat16 [32, 16, 32, 384], P('ra', 'dec', 'freq')
The draws below stay inside these ranges and needn't reach their ends.
All inputs are finite; a program needn't handle non-finite values.
Results may differ from the reference program's by a relative error of at most 0.023.
Values may be sent and summed in bfloat16 or wider, within the bound.
No kernel may reach another device: no remote copies, remote signals or barrier semaphores. Data moves between devices by JAX's collectives and lax.ppermute only.
A program may use at most 64 MiB of HBM per device.

```python
import jax
import jax.numpy as jnp
from jax import lax

C = 192
HEADS = 6
MLP = 768
WIN = 8
NR = 64
ND = 32
NF = 64


def draw_tokens(key, part):
    key = jax.random.fold_in(key, 11)
    key_base, key_rows, key_cols = jax.random.split(key, 3)
    base = jax.random.normal(key_base, (NR, ND, NF, C), jnp.float32)
    row_log = jax.random.uniform(key_rows, (NR, ND, NF, 1), jnp.float32, jnp.log(0.3), jnp.log(3.0))
    col_log = jax.random.uniform(key_cols, (1, 1, 1, C), jnp.float32, jnp.log(0.5), jnp.log(2.0))
    return jnp.clip(base * jnp.exp(row_log) * jnp.exp(col_log), -12.0, 12.0).astype(jnp.bfloat16)


def draw_qkv_weight(key, part):
    key = jax.random.fold_in(key, 23)
    key_base = jax.random.fold_in(key, 0)
    base = jax.random.normal(key_base, (2, C, 3 * C), jnp.float32) * C ** (-0.5)
    return jnp.clip(base, -3.0, 3.0).astype(jnp.bfloat16)


def normal_values(own_key, extent, spread, limit, held_as=jnp.bfloat16):
    entries = spread * jax.random.normal(own_key, extent, jnp.float32)
    return jnp.clip(entries, min=-limit, max=limit).astype(held_as)


def setup_inputs(seed: int = 0) -> dict:
    key_list = jax.random.split(jax.random.key(seed), 10)
    return {
        "tokens": draw_tokens(jax.random.fold_in(key_list[9], 71), 0),
        "attn_gain": jnp.clip(1.0 + 0.18 * jax.random.normal(key_list[1], (2, C), jnp.float32), 0.1, 1.9),
        "qkv_weight": draw_qkv_weight(jax.random.fold_in(key_list[9], 71), 0),
        "out_weight": normal_values(key_list[3], (2, C, C), C ** -0.5, 0.4375),
        "mlp_gain": jnp.clip(1.0 + 0.18 * jax.random.normal(key_list[4], (2, C), jnp.float32), 0.1, 1.9),
        "up_weight": normal_values(key_list[5], (2, C, MLP), C ** -0.5, 0.4375),
        "down_weight": normal_values(key_list[6], (2, MLP, C), MLP ** -0.5, 0.21875),
        "merge_gain": jnp.clip(1.0 + 0.18 * jax.random.normal(key_list[7], (8 * C,), jnp.float32), 0.1, 1.9),
        "merge_weight": normal_values(key_list[8], (8 * C, 2 * C), (8 * C) ** -0.5, 0.15625),
    }


def layer_norm(values, norm_gain):
    row_mean = lax.optimization_barrier(jnp.mean(values, axis=-1, keepdims=True))
    centred = values - row_mean
    row_var = lax.optimization_barrier(jnp.mean(centred * centred, axis=-1, keepdims=True))
    return centred * lax.rsqrt(row_var + 1e-05) * norm_gain

def to_windows(volume):
    rows_ra, rows_dec, rows_freq, depth = volume.shape
    blocked = volume.reshape(rows_ra // WIN, WIN, rows_dec // WIN, WIN, rows_freq // WIN, WIN, depth)
    return blocked.transpose(0, 2, 4, 1, 3, 5, 6).reshape(-1, WIN * WIN * WIN, depth)

def from_windows(windows, rows_ra, rows_dec, rows_freq):
    depth = windows.shape[-1]
    blocked = windows.reshape(rows_ra // WIN, rows_dec // WIN, rows_freq // WIN, WIN, WIN, WIN, depth)
    return blocked.transpose(0, 3, 1, 4, 2, 5, 6).reshape(rows_ra, rows_dec, rows_freq, depth)

def window_block(window, labels, layer_params):
    attn_norm, qkv_mat, out_mat, mlp_norm, up_mat, down_mat = layer_params
    model_width = window.shape[-1]
    head_size = model_width // HEADS
    normed = layer_norm(window.astype(jnp.float32), attn_norm).astype(jnp.bfloat16)
    projected = jnp.dot(normed, qkv_mat, preferred_element_type=jnp.float32).astype(jnp.bfloat16)
    split_heads = projected.reshape(-1, 3, HEADS, head_size).astype(jnp.float32)
    scores = jnp.einsum('qhd,khd->hqk', split_heads[:, 0], split_heads[:, 1]) * head_size ** (-0.5)
    if labels is not None:
        allowed = labels[:, None] == labels[None, :]
        scores = jnp.where(allowed[None], scores, -1e+30)
    row_top = lax.optimization_barrier(jnp.max(scores, axis=-1, keepdims=True))
    exponent = jnp.exp(scores - row_top)
    weights_bf = (exponent / lax.optimization_barrier(jnp.sum(exponent, axis=-1, keepdims=True))).astype(jnp.bfloat16)
    attended = jnp.einsum('hqk,khd->qhd', weights_bf.astype(jnp.float32), split_heads[:, 2])
    attended = attended.astype(jnp.bfloat16).reshape(-1, model_width)
    resid = (window.astype(jnp.float32) + jnp.dot(attended, out_mat, preferred_element_type=jnp.float32)).astype(jnp.bfloat16)
    normed_two = layer_norm(resid.astype(jnp.float32), mlp_norm).astype(jnp.bfloat16)
    activ = jax.nn.gelu(jnp.dot(normed_two, up_mat, preferred_element_type=jnp.float32), approximate=False).astype(jnp.bfloat16)
    return (resid.astype(jnp.float32) + jnp.dot(activ, down_mat, preferred_element_type=jnp.float32)).astype(jnp.bfloat16)

def run_block(volume, layer_params, label_grid):
    rows_ra, rows_dec, rows_freq, depth = volume.shape
    windows = to_windows(volume)
    if label_grid is None:
        outputs = lax.map(lambda window: window_block(window, None, layer_params), windows)
    else:
        label_windows = to_windows(label_grid[..., None])[..., 0]
        outputs = lax.map(lambda window_pair: window_block(window_pair[0], window_pair[1], layer_params), (windows, label_windows))
    return from_windows(outputs, rows_ra, rows_dec, rows_freq)

def region(coord, total):
    return jnp.where(coord < total - WIN, 0, jnp.where(coord < total - WIN // 2, 1, 2)).astype(jnp.int32)

def region_labels(coord_ra, coord_dec, coord_freq, total_ra, total_dec, total_freq):
    label_ra = region(coord_ra, total_ra)[:, None, None]
    label_dec = region(coord_dec, total_dec)[None, :, None]
    label_freq = region(coord_freq, total_freq)[None, None, :]
    return (label_ra * 9 + label_dec * 3 + label_freq).astype(jnp.int32)

def merge_patches(volume, merge_gain, merge_weight):
    rows_ra, rows_dec, rows_freq, depth = volume.shape
    grouped = volume.reshape(rows_ra // 2, 2, rows_dec // 2, 2, rows_freq // 2, 2, depth)
    grouped = grouped.transpose(0, 2, 4, 1, 3, 5, 6).reshape(rows_ra // 2, rows_dec // 2, rows_freq // 2, 8 * depth)
    normed = layer_norm(grouped.astype(jnp.float32), merge_gain).astype(jnp.bfloat16)
    return jnp.dot(normed, merge_weight, preferred_element_type=jnp.float32).astype(jnp.bfloat16)

def pick_layer(layer_index, attn_gain, qkv_weight, out_weight, mlp_gain, up_weight, down_weight):
    return (attn_gain[layer_index], qkv_weight[layer_index], out_weight[layer_index], mlp_gain[layer_index], up_weight[layer_index], down_weight[layer_index])

def reference(tokens, attn_gain, qkv_weight, out_weight, mlp_gain, up_weight, down_weight, merge_gain, merge_weight):
    half_win = WIN // 2
    first_out = run_block(tokens, pick_layer(0, attn_gain, qkv_weight, out_weight, mlp_gain, up_weight, down_weight), None)
    shifted = jnp.roll(first_out, -half_win, axis=(0, 1, 2))
    label_grid = region_labels(jnp.arange(NR, dtype=jnp.int32), jnp.arange(ND, dtype=jnp.int32), jnp.arange(NF, dtype=jnp.int32), NR, ND, NF)
    second_out = run_block(shifted, pick_layer(1, attn_gain, qkv_weight, out_weight, mlp_gain, up_weight, down_weight), label_grid)
    restored = jnp.roll(second_out, half_win, axis=(0, 1, 2))
    return merge_patches(restored, merge_gain, merge_weight)
```

```python
import functools

import jax
import jax.numpy as jnp
from jax import lax
from jax.experimental import pallas as pl
from jax.experimental.pallas import tpu as pltpu
from jax.sharding import PartitionSpec as P

HEADS = 6
WIN = 8
HALF = WIN // 2
PAIR = 2 * WIN
TOKENS = WIN * WIN * WIN
LOG2E = 1.4426950408889634
SUM_LOW = 2.0**-80
SUM_HIGH = 2.0**100
FAR = -1e30
VMEM_LIMIT = 30 * 2**20
FIRST_LIMIT = 60 * 2**20

f32 = jnp.float32
bf16 = jnp.bfloat16


def dot_f32(a, b):
    return jnp.dot(a, b, preferred_element_type=f32)


def dot_nt(a, b):
    return lax.dot_general(a, b, (((1,), (1,)), ((), ())), preferred_element_type=f32)


def layer_norm(values, gain):
    mean = jnp.mean(values, axis=-1, keepdims=True)
    centred = values - mean
    var = jnp.mean(centred * centred, axis=-1, keepdims=True)
    return centred * lax.rsqrt(var + 1e-05) * gain


def split_mask(rows, width):
    lane = lax.broadcasted_iota(jnp.int32, (rows, 128), 1) - (width - 128)
    row = lax.broadcasted_iota(jnp.int32, (rows, 128), 0)
    late_ra = row // (rows // 2)
    late_dec = (row // (WIN * HALF)) % 2
    late_freq = 1 - (row % WIN) // HALF
    late = jnp.where(lane < 2, late_ra, jnp.where(lane < 4, late_dec, late_freq))
    outside = jnp.where(lane < 0, 1, jnp.where(lane < 6, 0, 1))
    same = jnp.where(lane % 2 == late, 1, 0)
    key_cols = jnp.where(outside + 1 - same == 0, 1.0, 0.0)
    query_cols = jnp.where(outside + same == 0, FAR, 0.0)
    return query_cols.astype(f32), key_cols.astype(f32)


def attention(normed, qkv, width, masks, chunk, safe):
    rows = normed.shape[0]
    head_size = width // HEADS
    projected = dot_f32(normed, qkv)
    q = projected[:, :256] * f32(head_size**-0.5 * LOG2E)
    k = projected[:, 256:512]
    if masks is not None:
        query_cols, key_cols, active = masks
        extra = lax.broadcasted_iota(jnp.int32, (1, 128), 1) >= width - 128
        q = jnp.concatenate(
            [q[:, :128], jnp.where(extra, query_cols * active, q[:, 128:])], axis=1
        )
        k = jnp.concatenate([k[:, :128], jnp.where(extra, key_cols, k[:, 128:])], axis=1)
    q, k, v = q.astype(bf16), k.astype(bf16), projected[:, 512:].astype(bf16)
    ones = jnp.ones((rows, 128), bf16)
    v_low = jnp.concatenate([v[:, :128], ones], axis=1)
    v_high = jnp.concatenate([ones, v[:, 128:]], axis=1)
    lane = lax.broadcasted_iota(jnp.int32, (1, 256), 1)
    low_heads = 128 // head_size
    outs = []
    bad = jnp.zeros((1, 128), f32)
    for start in range(0, rows, chunk):
        q_part = q[start : start + chunk]
        data = [None, None]
        total = [None, None]
        for head in range(HEADS):
            own = (lane >= head_size * head) & (lane < head_size * (head + 1))
            q_head = jnp.where(own | (lane >= width), q_part, jnp.zeros((), bf16))
            scores = dot_nt(q_head, k)
            if safe:
                scores = scores - jnp.max(scores, axis=-1, keepdims=True)
            weights = jnp.exp2(scores).astype(bf16)
            side = 0 if head < low_heads else 1
            both = dot_f32(weights, v_low if side == 0 else v_high)
            mine, other = both[:, :128], both[:, 128:]
            if side:
                mine, other = other, mine
            if data[side] is None:
                data[side], total[side] = mine, other
            else:
                lanes = own[:, 128 * side : 128 * side + 128]
                data[side] = jnp.where(lanes, mine, data[side])
                total[side] = jnp.where(lanes, other, total[side])
        if not safe:
            for t in total:
                fine = jnp.where((t >= SUM_LOW) & (t <= SUM_HIGH), f32(0), f32(1))
                bad = jnp.maximum(bad, jnp.max(fine, axis=0, keepdims=True))
        low = data[0] * pl.reciprocal(total[0], approx=True)
        high = data[1] * pl.reciprocal(total[1], approx=True)
        outs.append(jnp.concatenate([low, high[:, : width - 128]], axis=1).astype(bf16))
    return jnp.concatenate(outs, axis=0), bad


def window_blocks(windows, masks, weights, safe):
    attn_gain, qkv, out_w, mlp_gain, up_w, down_w = weights
    width = windows[0].shape[-1]
    chunk = 128 if safe else 256
    outs = []
    bad = jnp.zeros((1, 128), f32)

    def feed_forward(resid, normed):
        activ = dot_f32(normed, up_w)
        activ = (0.5 * activ * (1.0 + lax.erf(activ * f32(0.5**0.5)))).astype(bf16)
        return (resid + dot_f32(activ, down_w)).astype(bf16)

    normed = layer_norm(windows[0], attn_gain).astype(bf16)
    waiting = None
    for i, window in enumerate(windows):
        following = None
        if i + 1 < len(windows):
            following = layer_norm(windows[i + 1], attn_gain).astype(bf16)
        attended, bad_here = attention(
            normed, qkv, width, None if masks is None else masks[i], chunk, safe
        )
        bad = jnp.maximum(bad, bad_here)
        if waiting is not None:
            outs.append(feed_forward(*waiting))
        resid = (window + dot_f32(attended, out_w)).astype(bf16).astype(f32)
        waiting = (resid, layer_norm(resid, mlp_gain).astype(bf16))
        normed = following
    outs.append(feed_forward(*waiting))
    return outs, bad


def prepare(qkv_ref, down_ref, qkv_s, down_s):
    qkv = qkv_ref[...]
    width = qkv.shape[0]
    gap = jnp.zeros((width, 256 - width), bf16)
    parts = []
    for i in range(3):
        parts += [qkv[:, i * width : (i + 1) * width], gap]
    qkv_s[...] = jnp.concatenate(parts, axis=1)
    down_s[...] = down_ref[...].T


def first_kernel(layer, n_extra, x_ref, ag_ref, qkv_ref, out_ref, mg_ref, up_ref, down_ref, *rest):
    *outs_ref, qkv_s, down_s = rest[n_extra:]
    width = x_ref.shape[-1]
    prepare(qkv_ref, down_ref, qkv_s, down_s)
    row = lax.broadcasted_iota(jnp.int32, (1, WIN, 1), 1)

    def run(step, safe):
        x = x_ref[...].astype(f32).reshape(WIN * WIN, 2, WIN, width)
        windows = [x[:, i].reshape(TOKENS, width) for i in range(2)]
        weights = (
            ag_ref[layer : layer + 1],
            qkv_s[...],
            out_ref[...],
            mg_ref[layer : layer + 1],
            up_ref[...],
            down_s[...],
        )
        outs, bad = window_blocks(windows, None, weights, safe)
        outs = [out.astype(f32).reshape(WIN * WIN, 1, WIN, width) for out in outs]
        y = jnp.concatenate(outs, axis=1).reshape(WIN, WIN, PAIR, width)
        edge = outs[0].reshape(WIN, 2, 2, 2, WIN, width)
        near = edge[:, :, 0].reshape(-1, WIN, width)
        far = pltpu.roll(edge[:, :, 1].reshape(-1, WIN, width), HALF, 1)
        edge = jnp.where(row < HALF, near, far).reshape(WIN, HALF, WIN, width)
        late, early = slice(HALF, WIN), slice(HALF)
        for ref, value in zip(
            outs_ref, (y[late], y[early], y[late, early], y[early, early], edge[late], edge[early])
        ):
            ref[...] = value.astype(bf16)
        return bad

    run_all(1, run)


def run_all(n_steps, run):
    def body(step, bad):
        return jnp.maximum(bad, run(step, False))

    bad = jnp.zeros((1, 128), f32)
    bad = run(0, False) if n_steps == 1 else lax.fori_loop(0, n_steps, body, bad)

    @pl.when(jnp.max(bad) > 0)
    def _():
        @pl.loop(0, n_steps)
        def _(step):
            run(step, True)


def cost(n_windows, width, args):
    mult = sum(a.shape[1] * a.shape[2] for a in args if a.ndim == 3) + 2 * TOKENS * width
    return pl.CostEstimate(
        flops=16 * n_windows * TOKENS * mult,
        bytes_accessed=4 * n_windows * TOKENS * width,
        transcendentals=n_windows * TOKENS * TOKENS * HEADS,
    )


def weight_specs(layer, args, grid_rank):
    attn_gain, qkv, out_w, mlp_gain, up_w, down_t = args

    def whole(a):
        return pl.BlockSpec(a.shape, lambda *_: (0,) * a.ndim)

    def one(a):
        return pl.BlockSpec((None, *a.shape[1:]), lambda *_: (layer,) + (0,) * (a.ndim - 1))

    return [whole(attn_gain), one(qkv), one(out_w), whole(mlp_gain), one(up_w), one(down_t)]


def weight_scratch(args):
    _, qkv, _, _, _, down_t = args
    return [
        pltpu.VMEM((qkv.shape[1], 768), bf16),
        pltpu.VMEM((down_t.shape[2], down_t.shape[1]), bf16),
    ]


def whole_spec(shape):
    return pl.BlockSpec(shape, lambda *_: (0,) * len(shape))


def first_block(tokens, args, pair, row, extra, vmem):
    ra, _, _, width = tokens.shape
    shapes = [(HALF, WIN, PAIR, width)] * 2 + [(HALF, HALF, PAIR, width)] * 2
    shapes += [(HALF, HALF, WIN, width)] * 2
    return pl.pallas_call(
        functools.partial(first_kernel, 0, len(extra)),
        grid=(1,),
        in_specs=[
            pl.BlockSpec((ra, WIN, PAIR, width), lambda *_: (0, row, pair, 0)),
            *weight_specs(0, args, 1),
            *[pl.BlockSpec(memory_space=pl.ANY) for _ in extra],
        ],
        out_specs=[whole_spec(shape) for shape in shapes],
        out_shape=[jax.ShapeDtypeStruct(shape, bf16) for shape in shapes],
        scratch_shapes=weight_scratch(args),
        compiler_params=pltpu.CompilerParams(vmem_limit_bytes=vmem),
        cost_estimate=cost(2, width, args),
    )(tokens, *args, *extra)


def second_kernel(layer, columns, n_freq, n_dec, n_pairs, with_edge, n_done, *refs):
    take = iter(refs)
    pairs = [[[next(take) for _ in range(4)] for _ in range(n_dec)] for _ in range(n_pairs)]
    edges = [[next(take) for _ in range(4)] for _ in range(n_dec)] if with_edge else None
    ag_ref, qkv_ref, out_ref, mg_ref, up_ref, down_ref = [next(take) for _ in range(6)]
    merging = n_done > 0
    if merging:
        done_ref, gain_ref, merge_ref = [next(take) for _ in range(3)]
        g_ref = next(take)
    else:
        y_ref = next(take)
    qkv_s, down_s, xs, query_s, key_s = [next(take) for _ in range(5)]
    dec, width = n_dec * WIN, pairs[0][0][0].shape[-1]
    prepare(qkv_ref, down_ref, qkv_s, down_s)
    query_cols, key_cols = split_mask(TOKENS, width)
    query_s[...] = query_cols
    key_s[...] = key_cols
    row = lax.broadcasted_iota(jnp.int32, (1, 1, WIN, 1), 2)
    first_column = columns[0]
    first_pair = first_column // 2 if with_edge else 0

    for i in range(n_dec):
        for late_ra in range(2):
            for late_dec in range(2):
                here = i + late_dec
                pick = late_ra if here < n_dec else 2 + late_ra
                here = here % n_dec
                first = HALF * (1 - late_dec)
                parts = []
                for pair in pairs:
                    body = pair[here][pick][:, first : first + HALF].astype(f32)
                    parts += [body[:, :, :WIN], body[:, :, WIN:]]
                if with_edge:
                    end = edges[here][pick][:, first // 2 : first // 2 + 2].astype(f32)
                    end = end.reshape(-1, WIN, width)
                    end = [
                        part.reshape(HALF, 2, WIN, width)
                        for part in (end, pltpu.roll(end, HALF, 1))
                    ]
                    parts.append(jnp.concatenate(end, axis=1))
                for j in columns:
                    tile = jnp.where(row < HALF, parts[j + 1], parts[j])
                    xs[
                        j - first_column,
                        i,
                        HALF * late_ra : HALF * late_ra + HALF,
                        HALF * late_dec : HALF * late_dec + HALF,
                    ] = tile

    last_ra = (lax.axis_index("ra") == lax.axis_size("ra") - 1).astype(jnp.int32)
    last_dec = (lax.axis_index("dec") == lax.axis_size("dec") - 1).astype(jnp.int32)
    last_freq = (lax.axis_index("freq") == lax.axis_size("freq") - 1).astype(jnp.int32)
    lane = lax.broadcasted_iota(jnp.int32, (1, 128), 1) - (width - 128)

    def keep(out, i, j):
        out = out.reshape(WIN, HALF, 2, WIN, width)
        after = jnp.where(j == n_freq - 1, 0, j + 1)
        for v in range(2):
            for lanes, low in ((slice(128), 0), (slice(width - 128), 128)):
                kept = out[:, :, v, :, low : low + 128]
                place = (low // 128, v, slice(None), slice(i * HALF, i * HALF + HALF))
                z[(*place, after, slice(HALF), lanes)] = kept[:, :, :HALF]
                z[(*place, j, slice(HALF, WIN), lanes)] = kept[:, :, HALF:]

    def run(step, safe):
        weights = (
            ag_ref[layer : layer + 1],
            qkv_s[...],
            out_ref[...],
            mg_ref[layer : layer + 1],
            up_ref[...],
            down_s[...],
        )
        j = first_column + step
        on_freq = jnp.where(j == n_freq - 1, last_freq, 0)
        windows, masks = [], []
        for i in range(n_dec):
            windows.append(xs[step, i].reshape(TOKENS, width))
            on_dec = last_dec if i == n_dec - 1 else 0
            on = jnp.where(lane < 2, last_ra, jnp.where(lane < 4, on_dec, on_freq))
            masks.append((query_s[...], key_s[...], on.astype(f32)))
        outs, bad = window_blocks(windows, masks, weights, safe)
        for i in range(n_dec):
            if merging:
                keep(outs[i].astype(f32), i, j)
            else:
                y_ref[step, i] = outs[i]
        return bad

    if merging:
        z = next(take)
        for j in range(n_done):
            for i in range(n_dec):
                keep(done_ref[j, i].astype(f32), i, j)
    run_all(len(columns), run)
    if not merging:
        return

    out_ra, out_dec, out_freq = WIN // 2, dec // 2, n_freq * HALF
    lines = z.shape[1] * z.shape[2] * z.shape[3] * n_freq * WIN
    flat = z.reshape(2 * lines, 128)
    groups = []
    for w in range(2):
        low = flat[pl.ds(w, lines // 2, stride=2), :]
        high = flat[pl.ds(lines + w, lines // 2, stride=2), :]
        picked = jnp.concatenate([low, high[:, : width - 128]], axis=1)
        groups.append(picked.reshape(2, out_ra, 2, out_dec * out_freq, width))
    merge_in = [
        groups[w][v, :, u].reshape(-1, width) for u in range(2) for v in range(2) for w in range(2)
    ]
    total = merge_in[0]
    for part in merge_in[1:]:
        total = total + part
    mean = jnp.sum(total, axis=-1, keepdims=True) * f32(1 / (8 * width))
    centred = [part - mean for part in merge_in]
    total = centred[0] * centred[0]
    for part in centred[1:]:
        total = total + part * part
    scale = lax.rsqrt(jnp.sum(total, axis=-1, keepdims=True) * f32(1 / (8 * width)) + 1e-05)
    merged = None
    for n, part in enumerate(centred):
        normed = (part * scale * gain_ref[n : n + 1]).astype(bf16)
        term = dot_f32(normed, merge_ref[n * width : (n + 1) * width])
        merged = term if merged is None else merged + term
    merged = merged.reshape(out_ra, out_dec, out_freq, -1)
    g_ref[...] = merged.astype(bf16)


def second_block(columns, n_freq, n_dec, pairs, edges, args, merge=None):
    width = pairs[0][0][0].shape[-1]
    dec = n_dec * WIN
    groups = pairs + ([edges] if edges else [])
    inputs = [part for group in groups for parts in group for part in parts]
    specs = [whole_spec(p.shape) for p in inputs] + weight_specs(1, args, 1)
    inputs += args
    scratch = [
        *weight_scratch(args),
        pltpu.VMEM((len(columns), n_dec, WIN, WIN, WIN, width), f32),
        pltpu.VMEM((TOKENS, 128), f32),
        pltpu.VMEM((TOKENS, 128), f32),
    ]
    n_done = 0
    if merge is None:
        shapes = [(len(columns), n_dec, TOKENS, width)]
    else:
        done, gain, merge_weight = merge
        n_done = done.shape[0]
        extra = [done, gain.reshape(8, width), merge_weight]
        inputs += extra
        specs += [whole_spec(e.shape) for e in extra]
        shapes = [(HALF, dec // 2, n_freq * HALF, merge_weight.shape[1])]
        scratch.append(pltpu.VMEM((2, 2, WIN, dec // 2, n_freq, WIN, 128), f32))
    return pl.pallas_call(
        functools.partial(
            second_kernel, 1, columns, n_freq, n_dec, len(pairs), edges is not None, n_done
        ),
        grid=(1,),
        in_specs=specs,
        out_specs=[whole_spec(shape) for shape in shapes],
        out_shape=[jax.ShapeDtypeStruct(shape, bf16) for shape in shapes],
        scratch_shapes=scratch,
        compiler_params=pltpu.CompilerParams(vmem_limit_bytes=VMEM_LIMIT),
        cost_estimate=cost(len(columns) * n_dec, width, args),
    )(*inputs)


def send(value, steps):
    axes = tuple(steps)
    sizes = [lax.axis_size(axis) for axis in axes]
    total = 1
    for size in sizes:
        total *= size
    pairs = []
    for source in range(total):
        rest, coords = source, []
        for size in reversed(sizes):
            coords.insert(0, rest % size)
            rest //= size
        target = 0
        for axis, size, coord in zip(axes, sizes, coords):
            target = target * size + (coord - steps[axis]) % size
        pairs.append((source, target))
    return lax.ppermute(value, axes, pairs)


def on_device(
    tokens,
    attn_gain,
    qkv_weight,
    out_weight,
    mlp_gain,
    up_weight,
    down_weight,
    merge_gain,
    merge_weight,
):
    args = (
        attn_gain,
        qkv_weight,
        out_weight,
        mlp_gain,
        up_weight,
        jnp.swapaxes(down_weight, 1, 2),
    )
    n_dec, n_freq = tokens.shape[1] // WIN, tokens.shape[2] // WIN
    to_ra, to_dec, to_freq = {"ra": 1}, {"dec": 1}, {"freq": 1}

    def with_halo(rows):
        out = [[late, send(early, to_ra)] for late, early, *_ in rows]
        late_dec, early_dec = rows[0][2:]
        dec_parts = [send(late_dec, to_dec), send(early_dec, {**to_ra, **to_dec})]
        return [row + dec_parts for row in out]

    pairs, extra = [], []
    for pair in range(n_freq // 2):
        rows = []
        for row in range(n_dec):
            limit = FIRST_LIMIT if pair == row == 0 else VMEM_LIMIT
            wait = extra if row == n_dec - 1 else []
            rows.append(first_block(tokens, args, pair, row, wait, limit))
        pairs.append(with_halo([row[:4] for row in rows]))
        if pair == 0:
            ends = [[send(edge, to_freq) for edge in row[4:]] for row in rows]
            extra = [*pairs[0][0][2:], pairs[0][0][1], *[edge for row in ends for edge in row]]
    late_end, early_end = ends[0]
    edges = with_halo([[*row, late_end[:, :2], early_end[:, :2]] for row in ends])
    (done,) = second_block([0], n_freq, n_dec, pairs[:1], None, args)
    (grid,) = second_block(
        list(range(1, n_freq)), n_freq, n_dec, pairs, edges, args, (done, merge_gain, merge_weight)
    )
    q = HALF // 2
    incoming = send(grid[-q:], {"ra": -1})
    grid = jnp.concatenate([incoming, grid[:-q]], axis=0)
    incoming = send(grid[:, -q:], {"dec": -1})
    grid = jnp.concatenate([incoming, grid[:, :-q]], axis=1)
    incoming = send(grid[:, :, :q], {"freq": -1})
    return jnp.concatenate([incoming, grid[:, :, q:]], axis=2)


def solution(mesh):
    placed = (P("ra", "dec", "freq", None), P(), P(), P(), P(), P(), P(), P(), P())
    return jax.shard_map(
        on_device,
        mesh=mesh,
        in_specs=placed,
        out_specs=P("ra", "dec", "freq", None),
        check_vma=False,
    )
```

```python
import functools

import jax
import jax.numpy as jnp
from jax import lax
from jax.experimental import pallas as pl
from jax.experimental.pallas import tpu as pltpu
from jax.sharding import PartitionSpec as P

HEADS = 6
WIN = 8
HALF = WIN // 2
PAIR = 2 * WIN
TOKENS = WIN * WIN * WIN
LOG2E = 1.4426950408889634
SUM_LOW = 2.0**-80
SUM_HIGH = 2.0**100
FAR = -1e30
VMEM_LIMIT = 26 * 2**20
FIRST_LIMIT = 60 * 2**20

f32 = jnp.float32
bf16 = jnp.bfloat16


def dot_f32(a, b):
    return jnp.dot(a, b, preferred_element_type=f32)


def dot_nt(a, b):
    return lax.dot_general(a, b, (((1,), (1,)), ((), ())), preferred_element_type=f32)


def layer_norm(values, gain):
    mean = jnp.mean(values, axis=-1, keepdims=True)
    centred = values - mean
    var = jnp.mean(centred * centred, axis=-1, keepdims=True)
    return centred * lax.rsqrt(var + 1e-05) * gain


def split_mask(rows, width):
    lane = lax.broadcasted_iota(jnp.int32, (rows, 128), 1) - (width - 128)
    row = lax.broadcasted_iota(jnp.int32, (rows, 128), 0)
    late_ra = row // (rows // 2)
    late_dec = (row // (WIN * HALF)) % 2
    late_freq = 1 - (row % WIN) // HALF
    late = jnp.where(lane < 2, late_ra, jnp.where(lane < 4, late_dec, late_freq))
    outside = jnp.where(lane < 0, 1, jnp.where(lane < 6, 0, 1))
    same = jnp.where(lane % 2 == late, 1, 0)
    key_cols = jnp.where(outside + 1 - same == 0, 1.0, 0.0)
    query_cols = jnp.where(outside + same == 0, FAR, 0.0)
    return query_cols.astype(f32), key_cols.astype(f32)


def mask_lanes(part, cols, width):
    extra = lax.broadcasted_iota(jnp.int32, (1, 128), 1) >= width - 128
    return jnp.concatenate([part[:, :128], jnp.where(extra, cols, part[:, 128:])], axis=1)


def value_parts(v):
    ones = jnp.ones((v.shape[0], 128), bf16)
    return jnp.concatenate([v[:, :128], ones], axis=1), jnp.concatenate([ones, v[:, 128:]], axis=1)


def attend(q_part, k, v_parts, width, safe):
    head_size = width // HEADS
    scale = f32(head_size**-0.5 * LOG2E)
    lane = lax.broadcasted_iota(jnp.int32, (1, 256), 1)
    data = [None, None]
    total = [None, None]
    for head in range(HEADS):
        own = (lane >= head_size * head) & (lane < head_size * (head + 1))
        q_head = jnp.where(own | (lane >= width), q_part, jnp.zeros((), bf16))
        scores = dot_nt(q_head, k)
        if safe:
            scores = scores - jnp.max(scores, axis=-1, keepdims=True)
        weights = jnp.exp2(scores * scale).astype(bf16)
        side = 0 if head < 128 // head_size else 1
        both = dot_f32(weights, v_parts[side])
        mine, other = both[:, :128], both[:, 128:]
        if side:
            mine, other = other, mine
        if data[side] is None:
            data[side], total[side] = mine, other
        else:
            lanes = own[:, 128 * side : 128 * side + 128]
            data[side] = jnp.where(lanes, mine, data[side])
            total[side] = jnp.where(lanes, other, total[side])
    low = data[0] * pl.reciprocal(total[0], approx=True)
    high = data[1] * pl.reciprocal(total[1], approx=True)
    return jnp.concatenate([low, high[:, : width - 128]], axis=1).astype(bf16), total


def attention(normed, qkv, width, masks, chunk):
    projected = dot_f32(normed, qkv)
    q = projected[:, :256]
    k = projected[:, 256:512]
    if masks is not None:
        query_cols, key_cols, active = masks
        q = mask_lanes(q, query_cols * active, width)
        k = mask_lanes(k, key_cols, width)
    q, k, v = q.astype(bf16), k.astype(bf16), projected[:, 512:].astype(bf16)
    v_parts = value_parts(v)
    outs = []
    bad = jnp.zeros((1, 128), f32)
    for start in range(0, normed.shape[0], chunk):
        out, totals = attend(q[start : start + chunk], k, v_parts, width, False)
        outs.append(out)
        for t in totals:
            fine = jnp.where((t >= SUM_LOW) & (t <= SUM_HIGH), f32(0), f32(1))
            bad = jnp.maximum(bad, jnp.max(fine, axis=0, keepdims=True))
    return jnp.concatenate(outs, axis=0), bad


def feed_forward(resid, normed, up_w, down_w):
    activ = dot_f32(normed, up_w)
    activ = (0.5 * activ * (1.0 + lax.erf(activ * f32(0.5**0.5)))).astype(bf16)
    return (resid + dot_f32(activ, down_w)).astype(bf16)


def safe_blocks(values, masks, weights, refs):
    attn_gain, qkv_s, out_ref, mlp_gain, up_ref, down_s = weights
    x_s, y_s, k_s, v_s, query_s, on_s = refs
    width = x_s.shape[-1]
    chunk = 128
    query_cols = jnp.zeros((TOKENS, 128), f32)
    key_cols = query_cols
    if masks is not None:
        query_cols, key_cols = masks[0][:2]
    query_s[...] = query_cols
    for n, value in enumerate(values):
        x_s[n] = value
        on_s[n] = masks[n][2] if masks is not None else jnp.zeros((1, 128), f32)

    @pl.loop(0, len(values))
    def _(n):
        normed = layer_norm(x_s[n], attn_gain).astype(bf16)
        k_s[...] = mask_lanes(dot_f32(normed, qkv_s[:, 256:512]), key_cols, width).astype(bf16)
        v_s[...] = dot_f32(normed, qkv_s[:, 512:]).astype(bf16)

        @pl.loop(0, TOKENS // chunk)
        def _(c):
            rows = pl.ds(pl.multiple_of(c * chunk, chunk), chunk)
            x = x_s[n, rows]
            q = dot_f32(layer_norm(x, attn_gain).astype(bf16), qkv_s[:, :256])
            q = mask_lanes(q, query_s[rows] * on_s[n], width).astype(bf16)
            attended, _ = attend(q, k_s[...], value_parts(v_s[...]), width, True)
            resid = (x + dot_f32(attended, out_ref[...])).astype(bf16).astype(f32)
            normed = layer_norm(resid, mlp_gain).astype(bf16)
            y_s[n, rows] = feed_forward(resid, normed, up_ref[...], down_s[...]).astype(f32)

    return [y_s[n].astype(bf16) for n in range(len(values))]


def window_blocks(windows, masks, weights):
    attn_gain, qkv_s, out_ref, mlp_gain, up_ref, down_s = weights
    width = windows[0].shape[-1]
    outs = []
    bad = jnp.zeros((1, 128), f32)
    normed = layer_norm(windows[0], attn_gain).astype(bf16)
    waiting = None
    for i, window in enumerate(windows):
        following = None
        if i + 1 < len(windows):
            following = layer_norm(windows[i + 1], attn_gain).astype(bf16)
        attended, bad_here = attention(
            normed, qkv_s[...], width, None if masks is None else masks[i], 256
        )
        bad = jnp.maximum(bad, bad_here)
        if waiting is not None:
            outs.append(feed_forward(*waiting, up_ref[...], down_s[...]))
        resid = (window + dot_f32(attended, out_ref[...])).astype(bf16).astype(f32)
        waiting = (resid, layer_norm(resid, mlp_gain).astype(bf16))
        normed = following
    outs.append(feed_forward(*waiting, up_ref[...], down_s[...]))
    return outs, bad


def run_blocks(load, masks, weights, safe_refs, store):
    outs, bad = window_blocks(load(), masks, weights)
    store(outs)

    @pl.when(jnp.max(bad) > 0)
    def _():
        store(safe_blocks(load(), masks, weights, safe_refs))


def prepare(qkv_ref, down_ref, qkv_s, down_s):
    qkv = qkv_ref[...]
    width = qkv.shape[0]
    gap = jnp.zeros((width, 256 - width), bf16)
    parts = []
    for i in range(3):
        parts += [qkv[:, i * width : (i + 1) * width], gap]
    qkv_s[...] = jnp.concatenate(parts, axis=1)
    down_s[...] = down_ref[...].T


def first_kernel(
    layer, row, edge_in, n_extra, x_ref, ag_ref, qkv_ref, out_ref, mg_ref, up_ref, down_ref, *rest
):
    rest = list(rest)
    edge_ref = rest.pop(0) if edge_in else None
    *outs_ref, qkv_s, down_s = rest[n_extra:-6]
    safe_refs = rest[-6:]
    width = x_ref.shape[-1]
    prepare(qkv_ref, down_ref, qkv_s, down_s)
    line = lax.broadcasted_iota(jnp.int32, (1, WIN, 1), 1)
    late, early = slice(HALF, WIN), slice(HALF)

    weights = (
        ag_ref[layer : layer + 1],
        qkv_s,
        out_ref,
        mg_ref[layer : layer + 1],
        up_ref,
        down_s,
    )

    def load():
        x = x_ref[...].astype(f32).reshape(WIN * WIN, 2, WIN, width)
        return [x[:, i].reshape(TOKENS, width) for i in range(2)]

    def store(outs):
        outs = [out.astype(f32).reshape(WIN * WIN, 1, WIN, width) for out in outs]
        y = jnp.concatenate(outs, axis=1).reshape(WIN, WIN, PAIR, width)
        values = [y[late], y[early]]
        if row == 0:
            values += [y[late, early], y[early, early]]
        for ref, value in zip(outs_ref, values):
            ref[:, : value.shape[1]] = value.astype(bf16)
        if not edge_in:
            edge = outs[0].reshape(WIN, 2, 2, 2, WIN, width)
            near = edge[:, :, 0].reshape(-1, WIN, width)
            far = pltpu.roll(edge[:, :, 1].reshape(-1, WIN, width), HALF, 1)
            edge = jnp.where(line < HALF, near, far).reshape(WIN, HALF, WIN, width)
            outs_ref[-1][...] = edge.astype(bf16)

    if edge_in:
        edge = edge_ref[...].astype(f32).reshape(WIN, 2, PAIR, width).astype(bf16)
        for i, ref in enumerate(outs_ref):
            part = edge[early] if i % 2 else edge[late]
            more = 2 if ref.shape[1] > WIN else 1
            ref[:, ref.shape[1] - more :] = part[:, :more]
    run_blocks(load, None, weights, safe_refs, store)


def cost(n_windows, width, args):
    mult = sum(a.shape[1] * a.shape[2] for a in args if a.ndim == 3) + 2 * TOKENS * width
    return pl.CostEstimate(
        flops=16 * n_windows * TOKENS * mult,
        bytes_accessed=4 * n_windows * TOKENS * width,
        transcendentals=n_windows * TOKENS * TOKENS * HEADS,
    )


def weight_specs(layer, args, grid_rank):
    attn_gain, qkv, out_w, mlp_gain, up_w, down_t = args

    def whole(a):
        return pl.BlockSpec(a.shape, lambda *_: (0,) * a.ndim)

    def one(a):
        return pl.BlockSpec((None, *a.shape[1:]), lambda *_: (layer,) + (0,) * (a.ndim - 1))

    return [whole(attn_gain), one(qkv), one(out_w), whole(mlp_gain), one(up_w), one(down_t)]


def weight_scratch(args):
    _, qkv, _, _, _, down_t = args
    return [
        pltpu.VMEM((qkv.shape[1], 768), bf16),
        pltpu.VMEM((down_t.shape[2], down_t.shape[1]), bf16),
        pltpu.VMEM((2, TOKENS, qkv.shape[1]), f32),
        pltpu.VMEM((2, TOKENS, qkv.shape[1]), f32),
        pltpu.VMEM((TOKENS, 256), bf16),
        pltpu.VMEM((TOKENS, 256), bf16),
        pltpu.VMEM((TOKENS, 128), f32),
        pltpu.VMEM((2, 1, 128), f32),
    ]


def whole_spec(shape):
    return pl.BlockSpec(shape, lambda *_: (0,) * len(shape))


def first_block(tokens, args, pair, row, edge, extra, vmem):
    ra, _, _, width = tokens.shape
    more = 0 if edge is None else 1
    shapes = [(HALF, WIN + 2 * more, PAIR, width)] * 2
    if row == 0:
        shapes += [(HALF, HALF + more, PAIR, width)] * 2
    if edge is None:
        shapes += [(ra, HALF, WIN, width)]
    edge = [] if edge is None else [edge]
    return pl.pallas_call(
        functools.partial(first_kernel, 0, row, bool(edge), len(extra)),
        grid=(1,),
        in_specs=[
            pl.BlockSpec((ra, WIN, PAIR, width), lambda *_: (0, row, pair, 0)),
            *weight_specs(0, args, 1),
            *[whole_spec(e.shape) for e in edge],
            *[pl.BlockSpec(memory_space=pl.ANY) for _ in extra],
        ],
        out_specs=[whole_spec(shape) for shape in shapes],
        out_shape=[jax.ShapeDtypeStruct(shape, bf16) for shape in shapes],
        scratch_shapes=weight_scratch(args),
        compiler_params=pltpu.CompilerParams(vmem_limit_bytes=vmem),
        cost_estimate=cost(2, width, args),
    )(tokens, *args, *edge, *extra)


def pieces_of(windows, n_freq):
    keys = {
        (column // 2, i + late_dec)
        for i, j in windows
        for column in (j, min(j + 1, n_freq - 1))
        for late_dec in range(2)
    }
    return sorted(keys)


def second_kernel(layer, windows, n_freq, n_dec, merge, n_extra, *refs):
    take = iter(refs)
    pieces = {key: [next(take) for _ in range(2)] for key in pieces_of(windows, n_freq)}
    ag_ref, qkv_ref, out_ref, mg_ref, up_ref, down_ref = [next(take) for _ in range(6)]
    if merge:
        earlier = [next(take) for _ in range(merge[0])]
        gain_ref, merge_ref = next(take), next(take)
    for _ in range(n_extra):
        next(take)
    y_ref = next(take)
    if merge:
        g_ref = next(take)
    qkv_s, down_s, *safe_refs = [next(take) for _ in range(8)]
    width = qkv_ref.shape[0]
    prepare(qkv_ref, down_ref, qkv_s, down_s)
    query_cols, key_cols = split_mask(TOKENS, width)
    line = lax.broadcasted_iota(jnp.int32, (1, 1, WIN, 1), 2)

    def part(i, column, late_ra, late_dec):
        pair = min(column // 2, n_freq // 2 - 1)
        ref = pieces[pair, i + late_dec][late_ra]
        if column < n_freq:
            first = HALF * (1 - late_dec)
            body = ref[:, first : first + HALF].astype(f32)
            return body[:, :, WIN * (column % 2) : WIN * (column % 2) + WIN]
        rows = ref.shape[1]
        count = 2 if rows > WIN else 1
        end = ref[:, rows - count :].astype(f32).reshape(HALF, 2 * count, WIN, width)
        first = 2 * (1 - late_dec)
        end = end[:, first : first + 2]
        turned = pltpu.roll(end.reshape(-1, WIN, width), HALF, 1)
        return jnp.concatenate([end, turned.reshape(HALF, 2, WIN, width)], axis=1)

    def assemble(i, j):
        rows = []
        for late_ra in range(2):
            quarters = []
            for late_dec in range(2):
                here, ahead = (part(i, j + k, late_ra, late_dec) for k in range(2))
                quarters.append(jnp.where(line < HALF, ahead, here))
            rows.append(jnp.concatenate(quarters, axis=1))
        return jnp.concatenate(rows, axis=0).reshape(TOKENS, width)

    last_ra = (lax.axis_index("ra") == lax.axis_size("ra") - 1).astype(jnp.int32)
    last_dec = (lax.axis_index("dec") == lax.axis_size("dec") - 1).astype(jnp.int32)
    last_freq = (lax.axis_index("freq") == lax.axis_size("freq") - 1).astype(jnp.int32)
    lane = lax.broadcasted_iota(jnp.int32, (1, 128), 1) - (width - 128)

    weights = (
        ag_ref[layer : layer + 1],
        qkv_s,
        out_ref,
        mg_ref[layer : layer + 1],
        up_ref,
        down_s,
    )
    masks = []
    for i, j in windows:
        on_dec = last_dec if i == n_dec - 1 else 0
        on_freq = last_freq if j == n_freq - 1 else 0
        on = jnp.where(lane < 2, last_ra, jnp.where(lane < 4, on_dec, on_freq))
        masks.append((query_cols, key_cols, on.astype(f32)))

    def load():
        return [assemble(i, j) for i, j in windows]

    def store(outs):
        for n, out in enumerate(outs):
            y_ref[n] = out

    run_blocks(load, masks, weights, safe_refs, store)
    if not merge:
        return

    z = next(take)
    n_earlier, layout = merge
    n_line, n_col = z.shape[3] // HALF, z.shape[4]
    for source, n, i, j in layout:
        out = (y_ref if source == n_earlier else earlier[source])[n].astype(f32)
        out = out.reshape(WIN, HALF, 2, WIN, width)
        for v in range(2):
            for lanes, low in ((slice(128), 0), (slice(width - 128), 128)):
                kept = out[:, :, v, :, low : low + 128]
                place = (low // 128, v, slice(None), slice(i * HALF, i * HALF + HALF))
                z[(*place, (j + 1) % n_col, slice(HALF), lanes)] = kept[:, :, :HALF]
                z[(*place, j, slice(HALF, WIN), lanes)] = kept[:, :, HALF:]
    lines = 2 * WIN * n_line * HALF * n_col * WIN
    flat = z.reshape(2 * lines, 128)
    groups = []
    for w in range(2):
        low = flat[pl.ds(w, lines // 2, stride=2), :]
        high = flat[pl.ds(lines + w, lines // 2, stride=2), :]
        picked = jnp.concatenate([low, high[:, : width - 128]], axis=1)
        groups.append(picked.reshape(2, HALF, 2, n_line * HALF * n_col * HALF, width))
    merge_in = [
        groups[w][v, :, u].reshape(-1, width) for u in range(2) for v in range(2) for w in range(2)
    ]
    total = merge_in[0]
    for value in merge_in[1:]:
        total = total + value
    mean = jnp.sum(total, axis=-1, keepdims=True) * f32(1 / (8 * width))
    centred = [value - mean for value in merge_in]
    total = centred[0] * centred[0]
    for value in centred[1:]:
        total = total + value * value
    scale = lax.rsqrt(jnp.sum(total, axis=-1, keepdims=True) * f32(1 / (8 * width)) + 1e-05)
    merged = None
    for n, value in enumerate(centred):
        normed = (value * scale * gain_ref[n : n + 1]).astype(bf16)
        term = dot_f32(normed, merge_ref[n * width : (n + 1) * width])
        merged = term if merged is None else merged + term
    if n_col == 1:
        for n in range(merged.shape[0] // HALF):
            place = (n // (n_line * HALF), n % (n_line * HALF))
            g_ref[place] = merged[n * HALF : n * HALF + HALF // 2].astype(bf16)
    else:
        g_ref[...] = merged.astype(bf16).reshape(g_ref.shape)


def second_block(windows, n_freq, n_dec, pieces, args, merge=None, extra=()):
    width = args[1].shape[1]
    inputs = [p for key in pieces_of(windows, n_freq) for p in pieces[key]]
    specs = [whole_spec(p.shape) for p in inputs] + weight_specs(1, args, 1)
    inputs += args
    scratch = weight_scratch(args)
    shapes = [(len(windows), TOKENS, width)]
    plan = None
    if merge is not None:
        gain, merge_weight, earlier, layout, (n_line, n_col) = merge
        more = [*earlier, gain.reshape(8, width), merge_weight]
        inputs += more
        specs += [whole_spec(m.shape) for m in more]
        plan = (len(earlier), layout)
        freq = HALF // 2 if n_col == 1 else n_col * HALF
        shapes.append((HALF, n_line * HALF, freq, merge_weight.shape[1]))
        scratch.append(pltpu.VMEM((2, 2, WIN, n_line * HALF, n_col, WIN, 128), f32))
    inputs += extra
    specs += [pl.BlockSpec(memory_space=pl.ANY) for _ in extra]
    return pl.pallas_call(
        functools.partial(second_kernel, 1, windows, n_freq, n_dec, plan, len(extra)),
        grid=(1,),
        in_specs=specs,
        out_specs=[whole_spec(shape) for shape in shapes],
        out_shape=[jax.ShapeDtypeStruct(shape, bf16) for shape in shapes],
        scratch_shapes=scratch,
        compiler_params=pltpu.CompilerParams(vmem_limit_bytes=VMEM_LIMIT),
        cost_estimate=cost(len(windows), width, args),
    )(*inputs)


def send(value, steps):
    axes = tuple(steps)
    sizes = [lax.axis_size(axis) for axis in axes]
    total = 1
    for size in sizes:
        total *= size
    pairs = []
    for source in range(total):
        rest, coords = source, []
        for size in reversed(sizes):
            coords.insert(0, rest % size)
            rest //= size
        target = 0
        for axis, size, coord in zip(axes, sizes, coords):
            target = target * size + (coord - steps[axis]) % size
        pairs.append((source, target))
    return lax.ppermute(value, axes, pairs)


def on_device(
    tokens,
    attn_gain,
    qkv_weight,
    out_weight,
    mlp_gain,
    up_weight,
    down_weight,
    merge_gain,
    merge_weight,
):
    args = (
        attn_gain,
        qkv_weight,
        out_weight,
        mlp_gain,
        up_weight,
        jnp.swapaxes(down_weight, 1, 2),
    )
    n_dec, n_freq = tokens.shape[1] // WIN, tokens.shape[2] // WIN
    to_ra, to_dec, to_freq = {"ra": 1}, {"dec": 1}, {"freq": 1}
    pieces, extra = {}, []
    ends = [None] * n_dec
    for pair in range(n_freq // 2):
        last = pair == n_freq // 2 - 1
        for row in range(n_dec):
            limit = FIRST_LIMIT if pair == row == 0 else VMEM_LIMIT
            wait = extra if last and row == n_dec - 1 else []
            late, early, *rest = first_block(
                tokens, args, pair, row, ends[row] if last else None, wait, limit
            )
            pieces[pair, row] = [late, send(early, to_ra)]
            if row == 0:
                late_dec, early_dec, *rest = rest
                pieces[pair, n_dec] = [
                    send(late_dec, to_dec),
                    send(early_dec, {**to_ra, **to_dec}),
                ]
            if pair == 0:
                ends[row] = send(rest[0], to_freq)
                if row == 0:
                    extra = [pieces[0, 0][1], *pieces[0, n_dec]]

    end = n_freq - 1
    (column_0,) = second_block([(0, 0), (1, 0)], n_freq, n_dec, pieces, args)
    column_end, edge = second_block(
        [(0, end), (1, end)],
        n_freq,
        n_dec,
        pieces,
        args,
        (merge_gain, merge_weight, [], [(0, 0, 0, 0), (0, 1, 1, 0)], (2, 1)),
    )
    edge = send(edge, {"freq": -1})

    def middle(i, extra):
        windows = [(i, j) for j in range(1, end)]
        layout = [(0, i, 0, 0), (1, i, 0, end)] + [(2, j - 1, 0, j) for j in range(1, end)]
        merge = (merge_gain, merge_weight, [column_0, column_end], layout, (1, n_freq))
        return second_block(windows, n_freq, n_dec, pieces, args, merge, extra)[1]

    q = HALF // 2
    high = middle(1, [])
    high = jnp.concatenate([edge[:, HALF:], high[:, :, q:]], axis=2)
    incoming = send(high[:, -q:], {"dec": -1})
    low = middle(0, [high])
    low = jnp.concatenate([edge[:, :HALF], low[:, :, q:]], axis=2)
    grid = jnp.concatenate([incoming, low, high[:, :-q]], axis=1)
    incoming = send(grid[-q:], {"ra": -1})
    return jnp.concatenate([incoming, grid[:-q]], axis=0)


def solution(mesh):
    placed = (P("ra", "dec", "freq", None), P(), P(), P(), P(), P(), P(), P(), P())
    return jax.shard_map(
        on_device,
        mesh=mesh,
        in_specs=placed,
        out_specs=P("ra", "dec", "freq", None),
        check_vma=False,
    )
```

```python
import functools

import jax
import jax.numpy as jnp
from jax import lax
from jax.experimental import pallas as pl
from jax.experimental.pallas import tpu as pltpu
from jax.sharding import PartitionSpec as P

HEADS = 6
WIN = 8
HALF = WIN // 2
PAIR = 2 * WIN
TOKENS = WIN * WIN * WIN
LOG2E = 1.4426950408889634
SUM_LOW = 2.0**-80
SUM_HIGH = 2.0**100
FAR = -1e30
VMEM_LIMIT = 26 * 2**20
FIRST_LIMIT = 60 * 2**20

f32 = jnp.float32
bf16 = jnp.bfloat16


def dot_f32(a, b):
    return jnp.dot(a, b, preferred_element_type=f32)


def dot_nt(a, b):
    return lax.dot_general(a, b, (((1,), (1,)), ((), ())), preferred_element_type=f32)


def layer_norm(values, gain):
    mean = jnp.mean(values, axis=-1, keepdims=True)
    centred = values - mean
    var = jnp.mean(centred * centred, axis=-1, keepdims=True)
    return centred * lax.rsqrt(var + 1e-05) * gain


def split_mask(rows, width):
    lane = lax.broadcasted_iota(jnp.int32, (rows, 128), 1) - (width - 128)
    row = lax.broadcasted_iota(jnp.int32, (rows, 128), 0)
    late_ra = row // (rows // 2)
    late_dec = (row // (WIN * HALF)) % 2
    late_freq = 1 - (row % WIN) // HALF
    late = jnp.where(lane < 2, late_ra, jnp.where(lane < 4, late_dec, late_freq))
    outside = jnp.where(lane < 0, 1, jnp.where(lane < 6, 0, 1))
    same = jnp.where(lane % 2 == late, 1, 0)
    key_cols = jnp.where(outside + 1 - same == 0, 1.0, 0.0)
    query_cols = jnp.where(outside + same == 0, FAR, 0.0)
    return query_cols.astype(f32), key_cols.astype(f32)


def mask_lanes(part, cols, width):
    extra = lax.broadcasted_iota(jnp.int32, (1, 128), 1) >= width - 128
    return jnp.concatenate([part[:, :128], jnp.where(extra, cols, part[:, 128:])], axis=1)


def value_parts(v):
    ones = jnp.ones((v.shape[0], 128), bf16)
    return jnp.concatenate([v[:, :128], ones], axis=1), jnp.concatenate([ones, v[:, 128:]], axis=1)


def attend(q_part, k, v_parts, width, safe):
    head_size = width // HEADS
    scale = f32(head_size**-0.5 * LOG2E)
    lane = lax.broadcasted_iota(jnp.int32, (1, 256), 1)
    data = [None, None]
    total = [None, None]
    for head in range(HEADS):
        own = (lane >= head_size * head) & (lane < head_size * (head + 1))
        q_head = jnp.where(own | (lane >= width), q_part, jnp.zeros((), bf16))
        scores = dot_nt(q_head, k)
        if safe:
            scores = scores - jnp.max(scores, axis=-1, keepdims=True)
        weights = jnp.exp2(scores * scale).astype(bf16)
        side = 0 if head < 128 // head_size else 1
        both = dot_f32(weights, v_parts[side])
        mine, other = both[:, :128], both[:, 128:]
        if side:
            mine, other = other, mine
        if data[side] is None:
            data[side], total[side] = mine, other
        else:
            lanes = own[:, 128 * side : 128 * side + 128]
            data[side] = jnp.where(lanes, mine, data[side])
            total[side] = jnp.where(lanes, other, total[side])
    low = data[0] * pl.reciprocal(total[0], approx=True)
    high = data[1] * pl.reciprocal(total[1], approx=True)
    return jnp.concatenate([low, high[:, : width - 128]], axis=1).astype(bf16), total


def attention(normed, qkv, width, masks, chunk):
    projected = dot_f32(normed, qkv)
    q = projected[:, :256]
    k = projected[:, 256:512]
    if masks is not None:
        query_cols, key_cols, active = masks
        q = mask_lanes(q, query_cols * active, width)
        k = mask_lanes(k, key_cols, width)
    q, k, v = q.astype(bf16), k.astype(bf16), projected[:, 512:].astype(bf16)
    v_parts = value_parts(v)
    outs = []
    bad = jnp.zeros((1, 128), f32)
    for start in range(0, normed.shape[0], chunk):
        out, totals = attend(q[start : start + chunk], k, v_parts, width, False)
        outs.append(out)
        for t in totals:
            fine = jnp.where((t >= SUM_LOW) & (t <= SUM_HIGH), f32(0), f32(1))
            bad = jnp.maximum(bad, jnp.max(fine, axis=0, keepdims=True))
    return jnp.concatenate(outs, axis=0), bad


def feed_forward(resid, normed, up_w, down_w):
    activ = dot_f32(normed, up_w)
    activ = (0.5 * activ * (1.0 + lax.erf(activ * f32(0.5**0.5)))).astype(bf16)
    return (resid + dot_f32(activ, down_w)).astype(bf16)


def safe_blocks(values, masks, weights, refs):
    attn_gain, qkv_s, out_ref, mlp_gain, up_ref, down_s = weights
    x_s, y_s, k_s, v_s, query_s, on_s = refs
    width = x_s.shape[-1]
    chunk = 128
    query_cols = jnp.zeros((TOKENS, 128), f32)
    key_cols = query_cols
    if masks is not None:
        query_cols, key_cols = masks[0][:2]
    query_s[...] = query_cols
    for n, value in enumerate(values):
        x_s[n] = value
        on_s[n] = masks[n][2] if masks is not None else jnp.zeros((1, 128), f32)

    @pl.loop(0, len(values))
    def _(n):
        normed = layer_norm(x_s[n], attn_gain).astype(bf16)
        k_s[...] = mask_lanes(dot_f32(normed, qkv_s[:, 256:512]), key_cols, width).astype(bf16)
        v_s[...] = dot_f32(normed, qkv_s[:, 512:]).astype(bf16)

        @pl.loop(0, TOKENS // chunk)
        def _(c):
            rows = pl.ds(pl.multiple_of(c * chunk, chunk), chunk)
            x = x_s[n, rows]
            q = dot_f32(layer_norm(x, attn_gain).astype(bf16), qkv_s[:, :256])
            q = mask_lanes(q, query_s[rows] * on_s[n], width).astype(bf16)
            attended, _ = attend(q, k_s[...], value_parts(v_s[...]), width, True)
            resid = (x + dot_f32(attended, out_ref[...])).astype(bf16).astype(f32)
            normed = layer_norm(resid, mlp_gain).astype(bf16)
            y_s[n, rows] = feed_forward(resid, normed, up_ref[...], down_s[...]).astype(f32)

    return [y_s[n].astype(bf16) for n in range(len(values))]


def window_blocks(windows, masks, weights):
    attn_gain, qkv_s, out_ref, mlp_gain, up_ref, down_s = weights
    width = windows[0].shape[-1]
    outs = []
    bad = jnp.zeros((1, 128), f32)
    normed = layer_norm(windows[0], attn_gain).astype(bf16)
    waiting = None
    for i, window in enumerate(windows):
        following = None
        if i + 1 < len(windows):
            following = layer_norm(windows[i + 1], attn_gain).astype(bf16)
        attended, bad_here = attention(
            normed, qkv_s[...], width, None if masks is None else masks[i], 256
        )
        bad = jnp.maximum(bad, bad_here)
        if waiting is not None:
            outs.append(feed_forward(*waiting, up_ref[...], down_s[...]))
        resid = (window + dot_f32(attended, out_ref[...])).astype(bf16).astype(f32)
        waiting = (resid, layer_norm(resid, mlp_gain).astype(bf16))
        normed = following
    outs.append(feed_forward(*waiting, up_ref[...], down_s[...]))
    return outs, bad


def run_blocks(load, masks, weights, safe_refs, store):
    outs, bad = window_blocks(load(), masks, weights)
    store(outs)

    @pl.when(jnp.max(bad) > 0)
    def _():
        store(safe_blocks(load(), masks, weights, safe_refs))


def prepare(qkv_ref, down_ref, qkv_s, down_s):
    qkv = qkv_ref[...]
    width = qkv.shape[0]
    gap = jnp.zeros((width, 256 - width), bf16)
    parts = []
    for i in range(3):
        parts += [qkv[:, i * width : (i + 1) * width], gap]
    qkv_s[...] = jnp.concatenate(parts, axis=1)
    down_s[...] = down_ref[...].T


def first_kernel(
    layer, row, carried, x_ref, ag_ref, qkv_ref, out_ref, mg_ref, up_ref, down_ref, *rest
):
    rest = list(rest)
    edge_ref, ahead_ref, before_ref = [rest.pop(0) if there else None for there in carried]
    *outs_ref, qkv_s, down_s = rest[:-6]
    safe_refs = rest[-6:]
    skip = 0 if before_ref is None else before_ref.shape[1]
    width = x_ref.shape[-1]
    prepare(qkv_ref, down_ref, qkv_s, down_s)
    line = lax.broadcasted_iota(jnp.int32, (1, WIN, 1), 1)
    late, early = slice(HALF, WIN), slice(HALF)

    weights = (
        ag_ref[layer : layer + 1],
        qkv_s,
        out_ref,
        mg_ref[layer : layer + 1],
        up_ref,
        down_s,
    )

    def load():
        x = x_ref[...].astype(f32).reshape(WIN * WIN, 2, WIN, width)
        return [x[:, i].reshape(TOKENS, width) for i in range(2)]

    def store(outs):
        outs = [out.astype(f32).reshape(WIN * WIN, 1, WIN, width) for out in outs]
        y = jnp.concatenate(outs, axis=1).reshape(WIN, WIN, PAIR, width)
        outs_ref[0][:, :WIN] = y[late].astype(bf16)
        outs_ref[1][:, skip : skip + WIN] = y[early].astype(bf16)
        if row == 0:
            outs_ref[2][:, :HALF] = y[:, early].astype(bf16)
        if edge_ref is None:
            edge = outs[0].reshape(WIN, 2, 2, 2, WIN, width)
            near = edge[:, :, 0].reshape(-1, WIN, width)
            far = pltpu.roll(edge[:, :, 1].reshape(-1, WIN, width), HALF, 1)
            edge = jnp.where(line < HALF, near, far).reshape(WIN, HALF, WIN, width)
            outs_ref[-1][...] = edge.astype(bf16)

    if before_ref is not None:
        outs_ref[1][:, :skip] = before_ref[...]
    if edge_ref is not None:
        edge = edge_ref[...].astype(f32).reshape(WIN, 2, PAIR, width).astype(bf16)
        outs_ref[0][:, WIN:] = edge[late]
        outs_ref[1][:, WIN : WIN + 2] = edge[early]
        if row == 0:
            outs_ref[2][:, HALF:] = edge[:, :1]
    if ahead_ref is not None:
        outs_ref[1][:, outs_ref[1].shape[1] - HALF :] = ahead_ref[early]
    run_blocks(load, None, weights, safe_refs, store)


def cost(n_windows, width, args):
    mult = sum(a.shape[1] * a.shape[2] for a in args if a.ndim == 3) + 2 * TOKENS * width
    return pl.CostEstimate(
        flops=16 * n_windows * TOKENS * mult,
        bytes_accessed=4 * n_windows * TOKENS * width,
        transcendentals=n_windows * TOKENS * TOKENS * HEADS,
    )


def weight_specs(layer, args, grid_rank):
    attn_gain, qkv, out_w, mlp_gain, up_w, down_t = args

    def whole(a):
        return pl.BlockSpec(a.shape, lambda *_: (0,) * a.ndim)

    def one(a):
        return pl.BlockSpec((None, *a.shape[1:]), lambda *_: (layer,) + (0,) * (a.ndim - 1))

    return [whole(attn_gain), one(qkv), one(out_w), whole(mlp_gain), one(up_w), one(down_t)]


def weight_scratch(args):
    _, qkv, _, _, _, down_t = args
    return [
        pltpu.VMEM((qkv.shape[1], 768), bf16),
        pltpu.VMEM((down_t.shape[2], down_t.shape[1]), bf16),
        pltpu.VMEM((2, TOKENS, qkv.shape[1]), f32),
        pltpu.VMEM((2, TOKENS, qkv.shape[1]), f32),
        pltpu.VMEM((TOKENS, 256), bf16),
        pltpu.VMEM((TOKENS, 256), bf16),
        pltpu.VMEM((TOKENS, 128), f32),
        pltpu.VMEM((2, 1, 128), f32),
    ]


def whole_spec(shape):
    return pl.BlockSpec(shape, lambda *_: (0,) * len(shape))


def first_block(tokens, args, pair, row, edge, ahead, before, vmem):
    ra, _, _, width = tokens.shape
    more = 0 if edge is None else 1
    carried = [edge, ahead, before]
    early = WIN + 2 * more + sum(HALF if c is ahead else WIN for c in carried[1:] if c is not None)
    shapes = [(HALF, WIN + 2 * more, PAIR, width), (HALF, early, PAIR, width)]
    if row == 0:
        shapes += [(ra, HALF + more, PAIR, width)]
    if edge is None:
        shapes += [(ra, HALF, WIN, width)]
    there = tuple(c is not None for c in carried)
    carried = [c for c in carried if c is not None]
    return pl.pallas_call(
        functools.partial(first_kernel, 0, row, there),
        grid=(1,),
        in_specs=[
            pl.BlockSpec((ra, WIN, PAIR, width), lambda *_: (0, row, pair, 0)),
            *weight_specs(0, args, 1),
            *[whole_spec(c.shape) for c in carried],
        ],
        out_specs=[whole_spec(shape) for shape in shapes],
        out_shape=[jax.ShapeDtypeStruct(shape, bf16) for shape in shapes],
        scratch_shapes=weight_scratch(args),
        compiler_params=pltpu.CompilerParams(vmem_limit_bytes=vmem),
        cost_estimate=cost(2, width, args),
    )(tokens, *args, *carried)


def pieces_of(windows, n_freq):
    keys = {
        (column // 2, i + late_dec)
        for i, j in windows
        for column in (j, min(j + 1, n_freq - 1))
        for late_dec in range(2)
    }
    return sorted(keys)


def second_kernel(layer, windows, n_freq, n_dec, places, n_arrays, merge, n_extra, *refs):
    take = iter(refs)
    arrays = [next(take) for _ in range(n_arrays)]
    ag_ref, qkv_ref, out_ref, mg_ref, up_ref, down_ref = [next(take) for _ in range(6)]
    if merge:
        earlier = [next(take) for _ in range(merge[0])]
        gain_ref, merge_ref = next(take), next(take)
    for _ in range(n_extra):
        next(take)
    y_ref = next(take)
    if merge:
        g_ref = next(take)
    qkv_s, down_s, *safe_refs = [next(take) for _ in range(8)]
    width = qkv_ref.shape[0]
    prepare(qkv_ref, down_ref, qkv_s, down_s)
    query_cols, key_cols = split_mask(TOKENS, width)
    line = lax.broadcasted_iota(jnp.int32, (1, 1, WIN, 1), 2)

    def part(i, column, late_ra, late_dec):
        pair = min(column // 2, n_freq // 2 - 1)
        array, plane, begin, rows = places[pair, i + late_dec][late_ra]
        ref, planes = arrays[array], slice(plane, plane + HALF)
        if column < n_freq:
            first = begin + HALF * (1 - late_dec)
            body = ref[planes, first : first + HALF].astype(f32)
            return body[:, :, WIN * (column % 2) : WIN * (column % 2) + WIN]
        count = 2 if rows > WIN else 1
        end = ref[planes, begin + rows - count : begin + rows].astype(f32)
        end = end.reshape(HALF, 2 * count, WIN, width)
        first = 2 * (1 - late_dec)
        end = end[:, first : first + 2]
        turned = pltpu.roll(end.reshape(-1, WIN, width), HALF, 1)
        return jnp.concatenate([end, turned.reshape(HALF, 2, WIN, width)], axis=1)

    def assemble(i, j):
        rows = []
        for late_ra in range(2):
            quarters = []
            for late_dec in range(2):
                here, ahead = (part(i, j + k, late_ra, late_dec) for k in range(2))
                quarters.append(jnp.where(line < HALF, ahead, here))
            rows.append(jnp.concatenate(quarters, axis=1))
        return jnp.concatenate(rows, axis=0).reshape(TOKENS, width)

    last_ra = (lax.axis_index("ra") == lax.axis_size("ra") - 1).astype(jnp.int32)
    last_dec = (lax.axis_index("dec") == lax.axis_size("dec") - 1).astype(jnp.int32)
    last_freq = (lax.axis_index("freq") == lax.axis_size("freq") - 1).astype(jnp.int32)
    lane = lax.broadcasted_iota(jnp.int32, (1, 128), 1) - (width - 128)

    weights = (
        ag_ref[layer : layer + 1],
        qkv_s,
        out_ref,
        mg_ref[layer : layer + 1],
        up_ref,
        down_s,
    )
    masks = []
    for i, j in windows:
        on_dec = last_dec if i == n_dec - 1 else 0
        on_freq = last_freq if j == n_freq - 1 else 0
        on = jnp.where(lane < 2, last_ra, jnp.where(lane < 4, on_dec, on_freq))
        masks.append((query_cols, key_cols, on.astype(f32)))

    def load():
        return [assemble(i, j) for i, j in windows]

    def store(outs):
        for n, out in enumerate(outs):
            y_ref[n] = out

    run_blocks(load, masks, weights, safe_refs, store)
    if not merge:
        return

    z = next(take)
    n_earlier, layout = merge
    n_line, n_col = z.shape[3] // HALF, z.shape[4]
    for source, n, i, j in layout:
        out = (y_ref if source == n_earlier else earlier[source])[n].astype(f32)
        out = out.reshape(WIN, HALF, 2, WIN, width)
        for v in range(2):
            for lanes, low in ((slice(128), 0), (slice(width - 128), 128)):
                kept = out[:, :, v, :, low : low + 128]
                place = (low // 128, v, slice(None), slice(i * HALF, i * HALF + HALF))
                z[(*place, (j + 1) % n_col, slice(HALF), lanes)] = kept[:, :, :HALF]
                z[(*place, j, slice(HALF, WIN), lanes)] = kept[:, :, HALF:]
    lines = 2 * WIN * n_line * HALF * n_col * WIN
    flat = z.reshape(2 * lines, 128)
    groups = []
    for w in range(2):
        low = flat[pl.ds(w, lines // 2, stride=2), :]
        high = flat[pl.ds(lines + w, lines // 2, stride=2), :]
        picked = jnp.concatenate([low, high[:, : width - 128]], axis=1)
        groups.append(picked.reshape(2, HALF, 2, n_line * HALF * n_col * HALF, width))
    merge_in = [
        groups[w][v, :, u].reshape(-1, width) for u in range(2) for v in range(2) for w in range(2)
    ]
    total = merge_in[0]
    for value in merge_in[1:]:
        total = total + value
    mean = jnp.sum(total, axis=-1, keepdims=True) * f32(1 / (8 * width))
    centred = [value - mean for value in merge_in]
    total = centred[0] * centred[0]
    for value in centred[1:]:
        total = total + value * value
    scale = lax.rsqrt(jnp.sum(total, axis=-1, keepdims=True) * f32(1 / (8 * width)) + 1e-05)
    merged = None
    for n, value in enumerate(centred):
        normed = (value * scale * gain_ref[:, n * width : (n + 1) * width]).astype(bf16)
        term = dot_f32(normed, merge_ref[n * width : (n + 1) * width])
        merged = term if merged is None else merged + term
    if n_col == 1:
        for n in range(merged.shape[0] // HALF):
            place = (n // (n_line * HALF), n % (n_line * HALF))
            g_ref[place] = merged[n * HALF : n * HALF + HALF // 2].astype(bf16)
    else:
        g_ref[...] = merged.astype(bf16).reshape(g_ref.shape)


def second_block(windows, n_freq, n_dec, pieces, args, merge=None, extra=()):
    width = args[1].shape[1]
    inputs, places = [], {}
    for key in pieces_of(windows, n_freq):
        places[key] = []
        for array, *place in pieces[key]:
            known = [n for n, other in enumerate(inputs) if other is array]
            if not known:
                known = [len(inputs)]
                inputs.append(array)
            places[key].append((known[0], *place))
    n_arrays = len(inputs)
    specs = [whole_spec(p.shape) for p in inputs] + weight_specs(1, args, 1)
    inputs += args
    scratch = weight_scratch(args)
    shapes = [(len(windows), TOKENS, width)]
    plan = None
    if merge is not None:
        gain, merge_weight, earlier, layout, (n_line, n_col) = merge
        more = [*earlier, gain.reshape(1, 8 * width), merge_weight]
        inputs += more
        specs += [whole_spec(m.shape) for m in more]
        plan = (len(earlier), layout)
        freq = HALF // 2 if n_col == 1 else n_col * HALF
        shapes.append((HALF, n_line * HALF, freq, merge_weight.shape[1]))
        scratch.append(pltpu.VMEM((2, 2, WIN, n_line * HALF, n_col, WIN, 128), f32))
    inputs += extra
    specs += [pl.BlockSpec(memory_space=pl.ANY) for _ in extra]
    return pl.pallas_call(
        functools.partial(
            second_kernel, 1, windows, n_freq, n_dec, places, n_arrays, plan, len(extra)
        ),
        grid=(1,),
        in_specs=specs,
        out_specs=[whole_spec(shape) for shape in shapes],
        out_shape=[jax.ShapeDtypeStruct(shape, bf16) for shape in shapes],
        scratch_shapes=scratch,
        compiler_params=pltpu.CompilerParams(vmem_limit_bytes=VMEM_LIMIT),
        cost_estimate=cost(len(windows), width, args),
    )(*inputs)


def send(value, steps):
    axes = tuple(steps)
    sizes = [lax.axis_size(axis) for axis in axes]
    total = 1
    for size in sizes:
        total *= size
    pairs = []
    for source in range(total):
        rest, coords = source, []
        for size in reversed(sizes):
            coords.insert(0, rest % size)
            rest //= size
        target = 0
        for axis, size, coord in zip(axes, sizes, coords):
            target = target * size + (coord - steps[axis]) % size
        pairs.append((source, target))
    return lax.ppermute(value, axes, pairs)


def on_device(
    tokens,
    attn_gain,
    qkv_weight,
    out_weight,
    mlp_gain,
    up_weight,
    down_weight,
    merge_gain,
    merge_weight,
):
    args = (
        attn_gain,
        qkv_weight,
        out_weight,
        mlp_gain,
        up_weight,
        jnp.swapaxes(down_weight, 1, 2),
    )
    n_dec, n_freq = tokens.shape[1] // WIN, tokens.shape[2] // WIN
    to_ra, to_dec, to_freq = {"ra": 1}, {"dec": 1}, {"freq": 1}
    pieces = {}
    ends, ahead = [None] * n_dec, None
    for pair in range(n_freq // 2):
        last = pair == n_freq // 2 - 1
        together = None
        for row in range(n_dec):
            limit = FIRST_LIMIT if pair == row == 0 else VMEM_LIMIT
            late, early, *rest = first_block(
                tokens,
                args,
                pair,
                row,
                ends[row] if last else None,
                ahead if last and row == 0 else None,
                together if not last and row > 0 else None,
                limit,
            )
            pieces[pair, row] = [(late, 0, 0, late.shape[1])]
            if row == 0:
                dec_part, *rest = rest
                ahead_now = send(dec_part, to_dec)
                pieces[pair, n_dec] = [(ahead_now, HALF, 0, ahead_now.shape[1])]
            if not last:
                ends[row] = send(rest[0], to_freq)
                together = early
                continue
            if row == n_dec - 1:
                early = jnp.concatenate([early, ahead_now[:HALF]], axis=1)
            moved = send(early, to_ra)
            rows = late.shape[1]
            pieces[pair, row].append((moved, 0, 0, rows))
            if row == 0 and ahead is not None:
                pieces[pair - 1, n_dec].append((moved, 0, rows, HALF))
            if row == n_dec - 1:
                pieces[pair, n_dec].append((moved, 0, rows, ahead_now.shape[1]))
        if not last:
            moved = send(together, to_ra)
            for row in range(n_dec):
                pieces[pair, row].append((moved, 0, row * WIN, WIN))
            ahead = ahead_now

    end = n_freq - 1
    (column_0,) = second_block([(0, 0), (1, 0)], n_freq, n_dec, pieces, args)
    column_end, edge = second_block(
        [(0, end), (1, end)],
        n_freq,
        n_dec,
        pieces,
        args,
        (merge_gain, merge_weight, [], [(0, 0, 0, 0), (0, 1, 1, 0)], (2, 1)),
    )
    edge = send(edge, {"freq": -1})

    def middle(i, extra):
        windows = [(i, j) for j in range(1, end)]
        layout = [(0, i, 0, 0), (1, i, 0, end)] + [(2, j - 1, 0, j) for j in range(1, end)]
        merge = (merge_gain, merge_weight, [column_0, column_end], layout, (1, n_freq))
        return second_block(windows, n_freq, n_dec, pieces, args, merge, extra)[1]

    q = HALF // 2
    high = middle(1, [])
    high = jnp.concatenate([edge[:, HALF:], high[:, :, q:]], axis=2)
    incoming = send(high[:, -q:], {"dec": -1})
    low = middle(0, [high])
    low = jnp.concatenate([edge[:, :HALF], low[:, :, q:]], axis=2)
    grid = jnp.concatenate([incoming, low, high[:, :-q]], axis=1)
    incoming = send(grid[-q:], {"ra": -1})
    return jnp.concatenate([incoming, grid[:-q]], axis=0)


def solution(mesh):
    placed = (P("ra", "dec", "freq", None), P(), P(), P(), P(), P(), P(), P(), P())
    return jax.shard_map(
        on_device,
        mesh=mesh,
        in_specs=placed,
        out_specs=P("ra", "dec", "freq", None),
        check_vma=False,
    )
```

```python
import functools

import jax
import jax.numpy as jnp
from jax import lax
from jax.experimental import pallas as pl
from jax.experimental.pallas import tpu as pltpu
from jax.sharding import PartitionSpec as P

HEADS = 6
WIN = 8
HALF = WIN // 2
PAIR = 2 * WIN
TOKENS = WIN * WIN * WIN
LOG2E = 1.4426950408889634
SUM_LOW = 2.0**-80
SUM_HIGH = 2.0**100
FAR = -1e30
VMEM_LIMIT = 26 * 2**20
FIRST_LIMIT = 60 * 2**20

f32 = jnp.float32
bf16 = jnp.bfloat16


def dot_f32(a, b):
    return jnp.dot(a, b, preferred_element_type=f32)


def dot_nt(a, b):
    return lax.dot_general(a, b, (((1,), (1,)), ((), ())), preferred_element_type=f32)


def layer_norm(values, gain):
    mean = jnp.mean(values, axis=-1, keepdims=True)
    centred = values - mean
    var = jnp.mean(centred * centred, axis=-1, keepdims=True)
    return centred * lax.rsqrt(var + 1e-05) * gain


def split_mask(rows, width):
    lane = lax.broadcasted_iota(jnp.int32, (rows, 128), 1) - (width - 128)
    row = lax.broadcasted_iota(jnp.int32, (rows, 128), 0)
    late_ra = row // (rows // 2)
    late_dec = (row // (WIN * HALF)) % 2
    late_freq = 1 - (row % WIN) // HALF
    late = jnp.where(lane < 2, late_ra, jnp.where(lane < 4, late_dec, late_freq))
    outside = jnp.where(lane < 0, 1, jnp.where(lane < 6, 0, 1))
    same = jnp.where(lane % 2 == late, 1, 0)
    key_cols = jnp.where(outside + 1 - same == 0, 1.0, 0.0)
    query_cols = jnp.where(outside + same == 0, FAR, 0.0)
    return query_cols.astype(f32), key_cols.astype(f32)


def mask_lanes(part, cols, width):
    extra = lax.broadcasted_iota(jnp.int32, (1, 128), 1) >= width - 128
    return jnp.concatenate([part[:, :128], jnp.where(extra, cols, part[:, 128:])], axis=1)


def value_parts(v):
    ones = jnp.ones((v.shape[0], 128), bf16)
    return jnp.concatenate([v[:, :128], ones], axis=1), jnp.concatenate([ones, v[:, 128:]], axis=1)


def attend(q_part, k, v_parts, width, safe):
    head_size = width // HEADS
    scale = f32(head_size**-0.5 * LOG2E)
    lane = lax.broadcasted_iota(jnp.int32, (1, 256), 1)
    data = [None, None]
    total = [None, None]
    for head in range(HEADS):
        own = (lane >= head_size * head) & (lane < head_size * (head + 1))
        q_head = jnp.where(own | (lane >= width), q_part, jnp.zeros((), bf16))
        scores = dot_nt(q_head, k)
        if safe:
            scores = scores - jnp.max(scores, axis=-1, keepdims=True)
        weights = jnp.exp2(scores * scale).astype(bf16)
        side = 0 if head < 128 // head_size else 1
        both = dot_f32(weights, v_parts[side])
        mine, other = both[:, :128], both[:, 128:]
        if side:
            mine, other = other, mine
        if data[side] is None:
            data[side], total[side] = mine, other
        else:
            lanes = own[:, 128 * side : 128 * side + 128]
            data[side] = jnp.where(lanes, mine, data[side])
            total[side] = jnp.where(lanes, other, total[side])
    low = data[0] * pl.reciprocal(total[0], approx=True)
    high = data[1] * pl.reciprocal(total[1], approx=True)
    return jnp.concatenate([low, high[:, : width - 128]], axis=1).astype(bf16), total


def attention(normed, qkv, width, masks, chunk):
    projected = dot_f32(normed, qkv)
    q = projected[:, :256]
    k = projected[:, 256:512]
    if masks is not None:
        query_cols, key_cols, active = masks
        q = mask_lanes(q, query_cols * active, width)
        k = mask_lanes(k, key_cols, width)
    q, k, v = q.astype(bf16), k.astype(bf16), projected[:, 512:].astype(bf16)
    v_parts = value_parts(v)
    outs = []
    bad = jnp.zeros((1, 128), f32)
    for start in range(0, normed.shape[0], chunk):
        out, totals = attend(q[start : start + chunk], k, v_parts, width, False)
        outs.append(out)
        for t in totals:
            fine = jnp.where((t >= SUM_LOW) & (t <= SUM_HIGH), f32(0), f32(1))
            bad = jnp.maximum(bad, jnp.max(fine, axis=0, keepdims=True))
    return jnp.concatenate(outs, axis=0), bad


def feed_forward(resid, normed, up_w, down_w):
    activ = dot_f32(normed, up_w)
    activ = (0.5 * activ * (1.0 + lax.erf(activ * f32(0.5**0.5)))).astype(bf16)
    return (resid + dot_f32(activ, down_w)).astype(bf16)


def safe_blocks(values, masks, weights, refs):
    attn_gain, qkv_s, out_ref, mlp_gain, up_ref, down_s = weights
    x_s, y_s, k_s, v_s, query_s, on_s = refs
    width = x_s.shape[-1]
    chunk = 128
    query_cols = jnp.zeros((TOKENS, 128), f32)
    key_cols = query_cols
    if masks is not None:
        query_cols, key_cols = masks[0][:2]
    query_s[...] = query_cols
    for n, value in enumerate(values):
        x_s[n] = value
        on_s[n] = masks[n][2] if masks is not None else jnp.zeros((1, 128), f32)

    @pl.loop(0, len(values))
    def _(n):
        normed = layer_norm(x_s[n], attn_gain).astype(bf16)
        k_s[...] = mask_lanes(dot_f32(normed, qkv_s[:, 256:512]), key_cols, width).astype(bf16)
        v_s[...] = dot_f32(normed, qkv_s[:, 512:]).astype(bf16)

        @pl.loop(0, TOKENS // chunk)
        def _(c):
            rows = pl.ds(pl.multiple_of(c * chunk, chunk), chunk)
            x = x_s[n, rows]
            q = dot_f32(layer_norm(x, attn_gain).astype(bf16), qkv_s[:, :256])
            q = mask_lanes(q, query_s[rows] * on_s[n], width).astype(bf16)
            attended, _ = attend(q, k_s[...], value_parts(v_s[...]), width, True)
            resid = (x + dot_f32(attended, out_ref[...])).astype(bf16).astype(f32)
            normed = layer_norm(resid, mlp_gain).astype(bf16)
            y_s[n, rows] = feed_forward(resid, normed, up_ref[...], down_s[...]).astype(f32)

    return [y_s[n].astype(bf16) for n in range(len(values))]


def window_blocks(windows, masks, weights):
    attn_gain, qkv_s, out_ref, mlp_gain, up_ref, down_s = weights
    width = windows[0].shape[-1]
    outs = []
    bad = jnp.zeros((1, 128), f32)
    normed = layer_norm(windows[0], attn_gain).astype(bf16)
    waiting = None
    for i, window in enumerate(windows):
        following = None
        if i + 1 < len(windows):
            following = layer_norm(windows[i + 1], attn_gain).astype(bf16)
        attended, bad_here = attention(
            normed, qkv_s[...], width, None if masks is None else masks[i], 256
        )
        bad = jnp.maximum(bad, bad_here)
        if waiting is not None:
            outs.append(feed_forward(*waiting, up_ref[...], down_s[...]))
        resid = (window + dot_f32(attended, out_ref[...])).astype(bf16).astype(f32)
        waiting = (resid, layer_norm(resid, mlp_gain).astype(bf16))
        normed = following
    outs.append(feed_forward(*waiting, up_ref[...], down_s[...]))
    return outs, bad


def run_blocks(load, masks, weights, safe_refs, store):
    outs, bad = window_blocks(load(), masks, weights)
    store(outs)

    @pl.when(jnp.max(bad) > 0)
    def _():
        store(safe_blocks(load(), masks, weights, safe_refs))


def prepare(qkv_ref, down_ref, qkv_s, down_s):
    qkv = qkv_ref[...]
    width = qkv.shape[0]
    gap = jnp.zeros((width, 256 - width), bf16)
    parts = []
    for i in range(3):
        parts += [qkv[:, i * width : (i + 1) * width], gap]
    qkv_s[...] = jnp.concatenate(parts, axis=1)
    down_s[...] = down_ref[...].T


def first_kernel(
    layer, row, carried, x_ref, ag_ref, qkv_ref, out_ref, mg_ref, up_ref, down_ref, *rest
):
    rest = list(rest)
    edge_ref, ahead_ref, before_ref = [rest.pop(0) if there else None for there in carried]
    *outs_ref, qkv_s, down_s = rest[:-6]
    safe_refs = rest[-6:]
    skip = 0 if before_ref is None else before_ref.shape[1]
    width = x_ref.shape[-1]
    prepare(qkv_ref, down_ref, qkv_s, down_s)
    line = lax.broadcasted_iota(jnp.int32, (1, WIN, 1), 1)
    late, early = slice(HALF, WIN), slice(HALF)

    weights = (
        ag_ref[layer : layer + 1],
        qkv_s,
        out_ref,
        mg_ref[layer : layer + 1],
        up_ref,
        down_s,
    )

    def load():
        x = x_ref[...].astype(f32).reshape(WIN * WIN, 2, WIN, width)
        return [x[:, i].reshape(TOKENS, width) for i in range(2)]

    def store(outs):
        outs = [out.astype(f32).reshape(WIN * WIN, 1, WIN, width) for out in outs]
        y = jnp.concatenate(outs, axis=1).reshape(WIN, WIN, PAIR, width)
        outs_ref[0][:, :WIN] = y[late].astype(bf16)
        outs_ref[1][:, skip : skip + WIN] = y[early].astype(bf16)
        if row == 0:
            outs_ref[2][:, :HALF] = y[:, early].astype(bf16)
        if edge_ref is None:
            edge = outs[0].reshape(WIN, 2, 2, 2, WIN, width)
            near = edge[:, :, 0].reshape(-1, WIN, width)
            far = pltpu.roll(edge[:, :, 1].reshape(-1, WIN, width), HALF, 1)
            edge = jnp.where(line < HALF, near, far).reshape(WIN, HALF, WIN, width)
            outs_ref[-1][...] = edge.astype(bf16)

    if before_ref is not None:
        outs_ref[1][:, :skip] = before_ref[...]
    if edge_ref is not None:
        edge = edge_ref[...].astype(f32).reshape(WIN, 2, PAIR, width).astype(bf16)
        outs_ref[0][:, WIN:] = edge[late]
        outs_ref[1][:, WIN : WIN + 2] = edge[early]
        if row == 0:
            outs_ref[2][:, HALF:] = edge[:, :1]
    if ahead_ref is not None:
        outs_ref[1][:, outs_ref[1].shape[1] - HALF :] = ahead_ref[early]
    run_blocks(load, None, weights, safe_refs, store)


def cost(n_windows, width, args):
    mult = sum(a.shape[1] * a.shape[2] for a in args if a.ndim == 3) + 2 * TOKENS * width
    return pl.CostEstimate(
        flops=16 * n_windows * TOKENS * mult,
        bytes_accessed=4 * n_windows * TOKENS * width,
        transcendentals=n_windows * TOKENS * TOKENS * HEADS,
    )


def weight_specs(layer, args, grid_rank):
    attn_gain, qkv, out_w, mlp_gain, up_w, down_t = args

    def whole(a):
        return pl.BlockSpec(a.shape, lambda *_: (0,) * a.ndim)

    def one(a):
        return pl.BlockSpec((None, *a.shape[1:]), lambda *_: (layer,) + (0,) * (a.ndim - 1))

    return [whole(attn_gain), one(qkv), one(out_w), whole(mlp_gain), one(up_w), one(down_t)]


def weight_scratch(args):
    _, qkv, _, _, _, down_t = args
    return [
        pltpu.VMEM((qkv.shape[1], 768), bf16),
        pltpu.VMEM((down_t.shape[2], down_t.shape[1]), bf16),
        pltpu.VMEM((2, TOKENS, qkv.shape[1]), f32),
        pltpu.VMEM((2, TOKENS, qkv.shape[1]), f32),
        pltpu.VMEM((TOKENS, 256), bf16),
        pltpu.VMEM((TOKENS, 256), bf16),
        pltpu.VMEM((TOKENS, 128), f32),
        pltpu.VMEM((2, 1, 128), f32),
    ]


def whole_spec(shape):
    return pl.BlockSpec(shape, lambda *_: (0,) * len(shape))


def first_block(tokens, args, pair, row, edge, ahead, before, vmem):
    ra, _, _, width = tokens.shape
    more = 0 if edge is None else 1
    carried = [edge, ahead, before]
    early = WIN + 2 * more + sum(HALF if c is ahead else WIN for c in carried[1:] if c is not None)
    shapes = [(HALF, WIN + 2 * more, PAIR, width), (HALF, early, PAIR, width)]
    if row == 0:
        shapes += [(ra, HALF + more, PAIR, width)]
    if edge is None:
        shapes += [(ra, HALF, WIN, width)]
    there = tuple(c is not None for c in carried)
    carried = [c for c in carried if c is not None]
    return pl.pallas_call(
        functools.partial(first_kernel, 0, row, there),
        grid=(1,),
        in_specs=[
            pl.BlockSpec((ra, WIN, PAIR, width), lambda *_: (0, row, pair, 0)),
            *weight_specs(0, args, 1),
            *[whole_spec(c.shape) for c in carried],
        ],
        out_specs=[whole_spec(shape) for shape in shapes],
        out_shape=[jax.ShapeDtypeStruct(shape, bf16) for shape in shapes],
        scratch_shapes=weight_scratch(args),
        compiler_params=pltpu.CompilerParams(vmem_limit_bytes=vmem),
        cost_estimate=cost(2, width, args),
    )(tokens, *args, *carried)


def pieces_of(windows, n_freq):
    keys = {
        (column // 2, i + late_dec)
        for i, j in windows
        for column in (j, min(j + 1, n_freq - 1))
        for late_dec in range(2)
    }
    return sorted(keys)


def second_kernel(layer, windows, n_freq, n_dec, places, n_arrays, merge, keeps, n_extra, *refs):
    take = iter(refs)
    arrays = [next(take) for _ in range(n_arrays)]
    ag_ref, qkv_ref, out_ref, mg_ref, up_ref, down_ref = [next(take) for _ in range(6)]
    if merge:
        earlier = [next(take) for _ in range(merge[0])]
        gain_ref, merge_ref = next(take), next(take)
    for _ in range(n_extra):
        next(take)
    y_ref = next(take) if keeps else None
    if merge:
        g_ref = next(take)
    qkv_s, down_s, *safe_refs = [next(take) for _ in range(8)]
    width = qkv_ref.shape[0]
    prepare(qkv_ref, down_ref, qkv_s, down_s)
    query_cols, key_cols = split_mask(TOKENS, width)
    line = lax.broadcasted_iota(jnp.int32, (1, 1, WIN, 1), 2)

    def part(i, column, late_ra, late_dec):
        pair = min(column // 2, n_freq // 2 - 1)
        array, plane, begin, rows = places[pair, i + late_dec][late_ra]
        ref, planes = arrays[array], slice(plane, plane + HALF)
        if column < n_freq:
            first = begin + HALF * (1 - late_dec)
            body = ref[planes, first : first + HALF].astype(f32)
            return body[:, :, WIN * (column % 2) : WIN * (column % 2) + WIN]
        count = 2 if rows > WIN else 1
        end = ref[planes, begin + rows - count : begin + rows].astype(f32)
        end = end.reshape(HALF, 2 * count, WIN, width)
        first = 2 * (1 - late_dec)
        end = end[:, first : first + 2]
        turned = pltpu.roll(end.reshape(-1, WIN, width), HALF, 1)
        return jnp.concatenate([end, turned.reshape(HALF, 2, WIN, width)], axis=1)

    def assemble(i, j):
        rows = []
        for late_ra in range(2):
            quarters = []
            for late_dec in range(2):
                here, ahead = (part(i, j + k, late_ra, late_dec) for k in range(2))
                quarters.append(jnp.where(line < HALF, ahead, here))
            rows.append(jnp.concatenate(quarters, axis=1))
        return jnp.concatenate(rows, axis=0).reshape(TOKENS, width)

    last_ra = (lax.axis_index("ra") == lax.axis_size("ra") - 1).astype(jnp.int32)
    last_dec = (lax.axis_index("dec") == lax.axis_size("dec") - 1).astype(jnp.int32)
    last_freq = (lax.axis_index("freq") == lax.axis_size("freq") - 1).astype(jnp.int32)
    lane = lax.broadcasted_iota(jnp.int32, (1, 128), 1) - (width - 128)

    weights = (
        ag_ref[layer : layer + 1],
        qkv_s,
        out_ref,
        mg_ref[layer : layer + 1],
        up_ref,
        down_s,
    )
    masks = []
    for i, j in windows:
        on_dec = last_dec if i == n_dec - 1 else 0
        on_freq = last_freq if j == n_freq - 1 else 0
        on = jnp.where(lane < 2, last_ra, jnp.where(lane < 4, on_dec, on_freq))
        masks.append((query_cols, key_cols, on.astype(f32)))

    own = []
    if merge:
        z = next(take)
        n_earlier, layout = merge
        n_line, n_col = z.shape[3] // HALF, z.shape[4]

        def put(out, i, j):
            out = out.astype(f32).reshape(WIN, HALF, 2, WIN, width)
            for v in range(2):
                for lanes, low in ((slice(128), 0), (slice(width - 128), 128)):
                    kept = out[:, :, v, :, low : low + 128]
                    place = (low // 128, v, slice(None), slice(i * HALF, i * HALF + HALF))
                    z[(*place, (j + 1) % n_col, slice(HALF), lanes)] = kept[:, :, :HALF]
                    z[(*place, j, slice(HALF, WIN), lanes)] = kept[:, :, HALF:]

        for source, n, i, j in layout:
            if source == n_earlier:
                own.append((n, i, j))
            else:
                put(earlier[source][n], i, j)

    def load():
        return [assemble(i, j) for i, j in windows]

    def store(outs):
        if keeps:
            for n, out in enumerate(outs):
                y_ref[n] = out
        for n, i, j in own:
            put(outs[n], i, j)

    run_blocks(load, masks, weights, safe_refs, store)
    if not merge:
        return

    lines = 2 * WIN * n_line * HALF * n_col * WIN
    flat = z.reshape(2 * lines, 128)
    groups = []
    for w in range(2):
        low = flat[pl.ds(w, lines // 2, stride=2), :]
        high = flat[pl.ds(lines + w, lines // 2, stride=2), :]
        picked = jnp.concatenate([low, high[:, : width - 128]], axis=1)
        groups.append(picked.reshape(2, HALF, 2, n_line * HALF * n_col * HALF, width))
    merge_in = [
        groups[w][v, :, u].reshape(-1, width) for u in range(2) for v in range(2) for w in range(2)
    ]
    total = merge_in[0]
    for value in merge_in[1:]:
        total = total + value
    mean = jnp.sum(total, axis=-1, keepdims=True) * f32(1 / (8 * width))
    centred = [value - mean for value in merge_in]
    total = centred[0] * centred[0]
    for value in centred[1:]:
        total = total + value * value
    scale = lax.rsqrt(jnp.sum(total, axis=-1, keepdims=True) * f32(1 / (8 * width)) + 1e-05)
    merged = None
    for n, value in enumerate(centred):
        normed = (value * scale * gain_ref[:, n * width : (n + 1) * width]).astype(bf16)
        term = dot_f32(normed, merge_ref[n * width : (n + 1) * width])
        merged = term if merged is None else merged + term
    if n_col == 1:
        for n in range(merged.shape[0] // HALF):
            place = (n // (n_line * HALF), n % (n_line * HALF))
            g_ref[place] = merged[n * HALF : n * HALF + HALF // 2].astype(bf16)
    else:
        g_ref[...] = merged.astype(bf16).reshape(g_ref.shape)


def second_block(windows, n_freq, n_dec, pieces, args, merge=None, keeps=True, extra=()):
    width = args[1].shape[1]
    inputs, places = [], {}
    for key in pieces_of(windows, n_freq):
        places[key] = []
        for array, *place in pieces[key]:
            known = [n for n, other in enumerate(inputs) if other is array]
            if not known:
                known = [len(inputs)]
                inputs.append(array)
            places[key].append((known[0], *place))
    n_arrays = len(inputs)
    specs = [whole_spec(p.shape) for p in inputs] + weight_specs(1, args, 1)
    inputs += args
    scratch = weight_scratch(args)
    shapes = [(len(windows), TOKENS, width)] if keeps else []
    plan = None
    if merge is not None:
        gain, merge_weight, earlier, layout, (n_line, n_col) = merge
        more = [*earlier, gain.reshape(1, 8 * width), merge_weight]
        inputs += more
        specs += [whole_spec(m.shape) for m in more]
        plan = (len(earlier), layout)
        freq = HALF // 2 if n_col == 1 else n_col * HALF
        shapes.append((HALF, n_line * HALF, freq, merge_weight.shape[1]))
        scratch.append(pltpu.VMEM((2, 2, WIN, n_line * HALF, n_col, WIN, 128), f32))
    inputs += extra
    specs += [pl.BlockSpec(memory_space=pl.ANY) for _ in extra]
    return pl.pallas_call(
        functools.partial(
            second_kernel, 1, windows, n_freq, n_dec, places, n_arrays, plan, keeps, len(extra)
        ),
        grid=(1,),
        in_specs=specs,
        out_specs=[whole_spec(shape) for shape in shapes],
        out_shape=[jax.ShapeDtypeStruct(shape, bf16) for shape in shapes],
        scratch_shapes=scratch,
        compiler_params=pltpu.CompilerParams(vmem_limit_bytes=VMEM_LIMIT),
        cost_estimate=cost(len(windows), width, args),
    )(*inputs)


def send(value, steps):
    axes = tuple(steps)
    sizes = [lax.axis_size(axis) for axis in axes]
    total = 1
    for size in sizes:
        total *= size
    pairs = []
    for source in range(total):
        rest, coords = source, []
        for size in reversed(sizes):
            coords.insert(0, rest % size)
            rest //= size
        target = 0
        for axis, size, coord in zip(axes, sizes, coords):
            target = target * size + (coord - steps[axis]) % size
        pairs.append((source, target))
    return lax.ppermute(value, axes, pairs)


def on_device(
    tokens,
    attn_gain,
    qkv_weight,
    out_weight,
    mlp_gain,
    up_weight,
    down_weight,
    merge_gain,
    merge_weight,
):
    args = (
        attn_gain,
        qkv_weight,
        out_weight,
        mlp_gain,
        up_weight,
        jnp.swapaxes(down_weight, 1, 2),
    )
    n_dec, n_freq = tokens.shape[1] // WIN, tokens.shape[2] // WIN
    to_ra, to_dec, to_freq = {"ra": 1}, {"dec": 1}, {"freq": 1}
    pieces = {}
    ends, ahead = [None] * n_dec, None
    for pair in range(n_freq // 2):
        last = pair == n_freq // 2 - 1
        together = None
        for row in range(n_dec):
            limit = FIRST_LIMIT if pair == row == 0 else VMEM_LIMIT
            late, early, *rest = first_block(
                tokens,
                args,
                pair,
                row,
                ends[row] if last else None,
                ahead if last and row == 0 else None,
                together if not last and row > 0 else None,
                limit,
            )
            pieces[pair, row] = [(late, 0, 0, late.shape[1])]
            if row == 0:
                dec_part, *rest = rest
                ahead_now = send(dec_part, to_dec)
                pieces[pair, n_dec] = [(ahead_now, HALF, 0, ahead_now.shape[1])]
            if not last:
                ends[row] = send(rest[0], to_freq)
                together = early
                continue
            if row == n_dec - 1:
                early = jnp.concatenate([early, ahead_now[:HALF]], axis=1)
            moved = send(early, to_ra)
            rows = late.shape[1]
            pieces[pair, row].append((moved, 0, 0, rows))
            if row == 0 and ahead is not None:
                pieces[pair - 1, n_dec].append((moved, 0, rows, HALF))
            if row == n_dec - 1:
                pieces[pair, n_dec].append((moved, 0, rows, ahead_now.shape[1]))
        if not last:
            moved = send(together, to_ra)
            for row in range(n_dec):
                pieces[pair, row].append((moved, 0, row * WIN, WIN))
            ahead = ahead_now

    end = n_freq - 1
    (column_0,) = second_block([(0, 0), (1, 0)], n_freq, n_dec, pieces, args)
    column_end, edge = second_block(
        [(0, end), (1, end)],
        n_freq,
        n_dec,
        pieces,
        args,
        (merge_gain, merge_weight, [], [(0, 0, 0, 0), (0, 1, 1, 0)], (2, 1)),
    )
    edge = send(edge, {"freq": -1})

    def middle(i, extra):
        windows = [(i, j) for j in range(1, end)]
        layout = [(0, i, 0, 0), (1, i, 0, end)] + [(2, j - 1, 0, j) for j in range(1, end)]
        merge = (merge_gain, merge_weight, [column_0, column_end], layout, (1, n_freq))
        return second_block(windows, n_freq, n_dec, pieces, args, merge, False, extra)[0]

    q = HALF // 2
    high = middle(1, [])
    high = jnp.concatenate([edge[:, HALF:], high[:, :, q:]], axis=2)
    incoming = send(high[:, -q:], {"dec": -1})
    low = middle(0, [high])
    low = jnp.concatenate([edge[:, :HALF], low[:, :, q:]], axis=2)
    grid = jnp.concatenate([incoming, low, high[:, :-q]], axis=1)
    incoming = send(grid[-q:], {"ra": -1})
    return jnp.concatenate([incoming, grid[:-q]], axis=0)


def solution(mesh):
    placed = (P("ra", "dec", "freq", None), P(), P(), P(), P(), P(), P(), P(), P())
    return jax.shard_map(
        on_device,
        mesh=mesh,
        in_specs=placed,
        out_specs=P("ra", "dec", "freq", None),
        check_vma=False,
    )
```

```python
import functools

import jax
import jax.numpy as jnp
from jax import lax
from jax.experimental import pallas as pl
from jax.experimental.pallas import tpu as pltpu
from jax.sharding import PartitionSpec as P

HEADS = 6
WIN = 8
HALF = WIN // 2
PAIR = 2 * WIN
TOKENS = WIN * WIN * WIN
LOG2E = 1.4426950408889634
SUM_LOW = 2.0**-80
SUM_HIGH = 2.0**100
FAR = -1e30
VMEM_LIMIT = 26 * 2**20
FIRST_LIMIT = 60 * 2**20

f32 = jnp.float32
bf16 = jnp.bfloat16


def dot_f32(a, b):
    return jnp.dot(a, b, preferred_element_type=f32)


def dot_nt(a, b):
    return lax.dot_general(a, b, (((1,), (1,)), ((), ())), preferred_element_type=f32)


def layer_norm(values, gain):
    mean = jnp.mean(values, axis=-1, keepdims=True)
    centred = values - mean
    var = jnp.mean(centred * centred, axis=-1, keepdims=True)
    return centred * lax.rsqrt(var + 1e-05) * gain


def split_mask(rows, width):
    lane = lax.broadcasted_iota(jnp.int32, (rows, 128), 1) - (width - 128)
    row = lax.broadcasted_iota(jnp.int32, (rows, 128), 0)
    late_ra = row // (rows // 2)
    late_dec = (row // (WIN * HALF)) % 2
    late_freq = 1 - (row % WIN) // HALF
    late = jnp.where(lane < 2, late_ra, jnp.where(lane < 4, late_dec, late_freq))
    outside = jnp.where(lane < 0, 1, jnp.where(lane < 6, 0, 1))
    same = jnp.where(lane % 2 == late, 1, 0)
    key_cols = jnp.where(outside + 1 - same == 0, 1.0, 0.0)
    query_cols = jnp.where(outside + same == 0, FAR, 0.0)
    return query_cols.astype(f32), key_cols.astype(f32)


def mask_lanes(part, cols, width):
    extra = lax.broadcasted_iota(jnp.int32, (1, 128), 1) >= width - 128
    return jnp.concatenate([part[:, :128], jnp.where(extra, cols, part[:, 128:])], axis=1)


def value_parts(v):
    ones = jnp.ones((v.shape[0], 128), bf16)
    return jnp.concatenate([v[:, :128], ones], axis=1), jnp.concatenate([ones, v[:, 128:]], axis=1)


def attend(q_part, k, v_parts, width, safe):
    head_size = width // HEADS
    scale = f32(head_size**-0.5 * LOG2E)
    lane = lax.broadcasted_iota(jnp.int32, (1, 256), 1)
    data = [None, None]
    total = [None, None]
    for head in range(HEADS):
        own = (lane >= head_size * head) & (lane < head_size * (head + 1))
        q_head = jnp.where(own | (lane >= width), q_part, jnp.zeros((), bf16))
        scores = dot_nt(q_head, k)
        if safe:
            scores = scores - jnp.max(scores, axis=-1, keepdims=True)
        weights = jnp.exp2(scores * scale).astype(bf16)
        side = 0 if head < 128 // head_size else 1
        both = dot_f32(weights, v_parts[side])
        mine, other = both[:, :128], both[:, 128:]
        if side:
            mine, other = other, mine
        if data[side] is None:
            data[side], total[side] = mine, other
        else:
            lanes = own[:, 128 * side : 128 * side + 128]
            data[side] = jnp.where(lanes, mine, data[side])
            total[side] = jnp.where(lanes, other, total[side])
    low = data[0] * pl.reciprocal(total[0], approx=True)
    high = data[1] * pl.reciprocal(total[1], approx=True)
    return jnp.concatenate([low, high[:, : width - 128]], axis=1).astype(bf16), total


def attention(normed, qkv, width, masks, chunk):
    projected = dot_f32(normed, qkv)
    q = projected[:, :256]
    k = projected[:, 256:512]
    if masks is not None:
        query_cols, key_cols, active = masks
        q = mask_lanes(q, query_cols * active, width)
        k = mask_lanes(k, key_cols, width)
    q, k, v = q.astype(bf16), k.astype(bf16), projected[:, 512:].astype(bf16)
    v_parts = value_parts(v)
    outs = []
    bad = jnp.zeros((1, 128), f32)
    for start in range(0, normed.shape[0], chunk):
        out, totals = attend(q[start : start + chunk], k, v_parts, width, False)
        outs.append(out)
        for t in totals:
            fine = jnp.where((t >= SUM_LOW) & (t <= SUM_HIGH), f32(0), f32(1))
            bad = jnp.maximum(bad, jnp.max(fine, axis=0, keepdims=True))
    return jnp.concatenate(outs, axis=0), bad


def feed_forward(resid, normed, up_w, down_w):
    activ = dot_f32(normed, up_w)
    activ = (0.5 * activ * (1.0 + lax.erf(activ * f32(0.5**0.5)))).astype(bf16)
    return (resid + dot_f32(activ, down_w)).astype(bf16)


def safe_blocks(values, masks, weights, refs):
    attn_gain, qkv_s, out_ref, mlp_gain, up_ref, down_s = weights
    x_s, y_s, k_s, v_s, query_s, on_s = refs
    width = x_s.shape[-1]
    chunk = 128
    query_cols = jnp.zeros((TOKENS, 128), f32)
    key_cols = query_cols
    if masks is not None:
        query_cols, key_cols = masks[0][:2]
    query_s[...] = query_cols
    for n, value in enumerate(values):
        x_s[n] = value
        on_s[n] = masks[n][2] if masks is not None else jnp.zeros((1, 128), f32)

    @pl.loop(0, len(values))
    def _(n):
        normed = layer_norm(x_s[n], attn_gain).astype(bf16)
        k_s[...] = mask_lanes(dot_f32(normed, qkv_s[:, 256:512]), key_cols, width).astype(bf16)
        v_s[...] = dot_f32(normed, qkv_s[:, 512:]).astype(bf16)

        @pl.loop(0, TOKENS // chunk)
        def _(c):
            rows = pl.ds(pl.multiple_of(c * chunk, chunk), chunk)
            x = x_s[n, rows]
            q = dot_f32(layer_norm(x, attn_gain).astype(bf16), qkv_s[:, :256])
            q = mask_lanes(q, query_s[rows] * on_s[n], width).astype(bf16)
            attended, _ = attend(q, k_s[...], value_parts(v_s[...]), width, True)
            resid = (x + dot_f32(attended, out_ref[...])).astype(bf16).astype(f32)
            normed = layer_norm(resid, mlp_gain).astype(bf16)
            y_s[n, rows] = feed_forward(resid, normed, up_ref[...], down_s[...]).astype(f32)

    return [y_s[n].astype(bf16) for n in range(len(values))]


def window_blocks(windows, masks, weights):
    attn_gain, qkv_s, out_ref, mlp_gain, up_ref, down_s = weights
    width = windows[0].shape[-1]
    outs = []
    bad = jnp.zeros((1, 128), f32)
    normed = layer_norm(windows[0], attn_gain).astype(bf16)
    waiting = None
    for i, window in enumerate(windows):
        following = None
        if i + 1 < len(windows):
            following = layer_norm(windows[i + 1], attn_gain).astype(bf16)
        attended, bad_here = attention(
            normed, qkv_s[...], width, None if masks is None else masks[i], 256
        )
        bad = jnp.maximum(bad, bad_here)
        if waiting is not None:
            outs.append(feed_forward(*waiting, up_ref[...], down_s[...]))
        resid = (window + dot_f32(attended, out_ref[...])).astype(bf16).astype(f32)
        waiting = (resid, layer_norm(resid, mlp_gain).astype(bf16))
        normed = following
    outs.append(feed_forward(*waiting, up_ref[...], down_s[...]))
    return outs, bad


def run_blocks(load, masks, weights, safe_refs, store):
    outs, bad = window_blocks(load(), masks, weights)
    store(outs)

    @pl.when(jnp.max(bad) > 0)
    def _():
        store(safe_blocks(load(), masks, weights, safe_refs))


def prepare(qkv_ref, down_ref, qkv_s, down_s):
    qkv = qkv_ref[...]
    width = qkv.shape[0]
    gap = jnp.zeros((width, 256 - width), bf16)
    parts = []
    for i in range(3):
        parts += [qkv[:, i * width : (i + 1) * width], gap]
    qkv_s[...] = jnp.concatenate(parts, axis=1)
    down_s[...] = down_ref[...].T


def first_kernel(
    layer, row, carried, x_ref, ag_ref, qkv_ref, out_ref, mg_ref, up_ref, down_ref, *rest
):
    rest = list(rest)
    edge_ref, ahead_ref, before_ref = [rest.pop(0) if there else None for there in carried]
    copied = rest.pop() if before_ref is not None else None
    *outs_ref, qkv_s, down_s = rest[:-6]
    safe_refs = rest[-6:]
    skip = 0 if before_ref is None else before_ref.shape[1]
    width = x_ref.shape[-1]
    if before_ref is not None:
        bring = pltpu.make_async_copy(before_ref, outs_ref[1].at[:, :skip], copied)
        bring.start()
    prepare(qkv_ref, down_ref, qkv_s, down_s)
    line = lax.broadcasted_iota(jnp.int32, (1, WIN, 1), 1)
    late, early = slice(HALF, WIN), slice(HALF)

    weights = (
        ag_ref[layer : layer + 1],
        qkv_s,
        out_ref,
        mg_ref[layer : layer + 1],
        up_ref,
        down_s,
    )

    def load():
        x = x_ref[...].astype(f32).reshape(WIN * WIN, 2, WIN, width)
        return [x[:, i].reshape(TOKENS, width) for i in range(2)]

    def store(outs):
        outs = [out.astype(f32).reshape(WIN * WIN, 1, WIN, width) for out in outs]
        y = jnp.concatenate(outs, axis=1).reshape(WIN, WIN, PAIR, width)
        outs_ref[0][:, :WIN] = y[late].astype(bf16)
        outs_ref[1][:, skip : skip + WIN] = y[early].astype(bf16)
        if row == 0:
            outs_ref[2][:, :HALF] = y[:, early].astype(bf16)
        if edge_ref is None:
            edge = outs[0].reshape(WIN, 2, 2, 2, WIN, width)
            near = edge[:, :, 0].reshape(-1, WIN, width)
            far = pltpu.roll(edge[:, :, 1].reshape(-1, WIN, width), HALF, 1)
            edge = jnp.where(line < HALF, near, far).reshape(WIN, HALF, WIN, width)
            outs_ref[-1][...] = edge.astype(bf16)

    if edge_ref is not None:
        edge = edge_ref[...].astype(f32).reshape(WIN, 2, PAIR, width).astype(bf16)
        outs_ref[0][:, WIN:] = edge[late]
        outs_ref[1][:, WIN : WIN + 2] = edge[early]
        if row == 0:
            outs_ref[2][:, HALF:] = edge[:, :1]
    if ahead_ref is not None:
        outs_ref[1][:, outs_ref[1].shape[1] - HALF :] = ahead_ref[early]
    run_blocks(load, None, weights, safe_refs, store)
    if before_ref is not None:
        bring.wait()


def cost(n_windows, width, args):
    mult = sum(a.shape[1] * a.shape[2] for a in args if a.ndim == 3) + 2 * TOKENS * width
    return pl.CostEstimate(
        flops=16 * n_windows * TOKENS * mult,
        bytes_accessed=4 * n_windows * TOKENS * width,
        transcendentals=n_windows * TOKENS * TOKENS * HEADS,
    )


def weight_specs(layer, args, grid_rank):
    attn_gain, qkv, out_w, mlp_gain, up_w, down_t = args

    def whole(a):
        return pl.BlockSpec(a.shape, lambda *_: (0,) * a.ndim)

    def one(a):
        return pl.BlockSpec((None, *a.shape[1:]), lambda *_: (layer,) + (0,) * (a.ndim - 1))

    return [whole(attn_gain), one(qkv), one(out_w), whole(mlp_gain), one(up_w), one(down_t)]


def weight_scratch(args):
    _, qkv, _, _, _, down_t = args
    return [
        pltpu.VMEM((qkv.shape[1], 768), bf16),
        pltpu.VMEM((down_t.shape[2], down_t.shape[1]), bf16),
        pltpu.VMEM((2, TOKENS, qkv.shape[1]), f32),
        pltpu.VMEM((2, TOKENS, qkv.shape[1]), f32),
        pltpu.VMEM((TOKENS, 256), bf16),
        pltpu.VMEM((TOKENS, 256), bf16),
        pltpu.VMEM((TOKENS, 128), f32),
        pltpu.VMEM((2, 1, 128), f32),
    ]


def whole_spec(shape):
    return pl.BlockSpec(shape, lambda *_: (0,) * len(shape))


def first_block(tokens, args, pair, row, edge, ahead, before, vmem):
    ra, _, _, width = tokens.shape
    more = 0 if edge is None else 1
    carried = [edge, ahead, before]
    early = WIN + 2 * more + sum(HALF if c is ahead else WIN for c in carried[1:] if c is not None)
    shapes = [(HALF, WIN + 2 * more, PAIR, width), (HALF, early, PAIR, width)]
    if row == 0:
        shapes += [(ra, HALF + more, PAIR, width)]
    if edge is None:
        shapes += [(ra, HALF, WIN, width)]
    there = tuple(c is not None for c in carried)
    carried = [c for c in carried if c is not None]
    return pl.pallas_call(
        functools.partial(first_kernel, 0, row, there),
        grid=(1,),
        in_specs=[
            pl.BlockSpec((ra, WIN, PAIR, width), lambda *_: (0, row, pair, 0)),
            *weight_specs(0, args, 1),
            *[
                pl.BlockSpec(memory_space=pltpu.HBM) if c is before else whole_spec(c.shape)
                for c in carried
            ],
        ],
        out_specs=[whole_spec(shape) for shape in shapes],
        out_shape=[jax.ShapeDtypeStruct(shape, bf16) for shape in shapes],
        scratch_shapes=weight_scratch(args)
        + ([] if before is None else [pltpu.SemaphoreType.DMA]),
        compiler_params=pltpu.CompilerParams(vmem_limit_bytes=vmem),
        cost_estimate=cost(2, width, args),
    )(tokens, *args, *carried)


def pieces_of(windows, n_freq):
    keys = {
        (column // 2, i + late_dec)
        for i, j in windows
        for column in (j, min(j + 1, n_freq - 1))
        for late_dec in range(2)
    }
    return sorted(keys)


def second_kernel(layer, windows, n_freq, n_dec, places, n_arrays, merge, keeps, n_extra, *refs):
    take = iter(refs)
    arrays = [next(take) for _ in range(n_arrays)]
    ag_ref, qkv_ref, out_ref, mg_ref, up_ref, down_ref = [next(take) for _ in range(6)]
    if merge:
        earlier = [next(take) for _ in range(merge[0])]
        gain_ref, merge_ref = next(take), next(take)
    for _ in range(n_extra):
        next(take)
    y_ref = next(take) if keeps else None
    if merge:
        g_ref = next(take)
    qkv_s, down_s, *safe_refs = [next(take) for _ in range(8)]
    width = qkv_ref.shape[0]
    prepare(qkv_ref, down_ref, qkv_s, down_s)
    query_cols, key_cols = split_mask(TOKENS, width)
    line = lax.broadcasted_iota(jnp.int32, (1, 1, WIN, 1), 2)

    def part(i, column, late_ra, late_dec):
        pair = min(column // 2, n_freq // 2 - 1)
        array, plane, begin, rows = places[pair, i + late_dec][late_ra]
        ref, planes = arrays[array], slice(plane, plane + HALF)
        if column < n_freq:
            first = begin + HALF * (1 - late_dec)
            body = ref[planes, first : first + HALF].astype(f32)
            return body[:, :, WIN * (column % 2) : WIN * (column % 2) + WIN]
        count = 2 if rows > WIN else 1
        end = ref[planes, begin + rows - count : begin + rows].astype(f32)
        end = end.reshape(HALF, 2 * count, WIN, width)
        first = 2 * (1 - late_dec)
        end = end[:, first : first + 2]
        turned = pltpu.roll(end.reshape(-1, WIN, width), HALF, 1)
        return jnp.concatenate([end, turned.reshape(HALF, 2, WIN, width)], axis=1)

    def assemble(i, j):
        rows = []
        for late_ra in range(2):
            quarters = []
            for late_dec in range(2):
                here, ahead = (part(i, j + k, late_ra, late_dec) for k in range(2))
                quarters.append(jnp.where(line < HALF, ahead, here))
            rows.append(jnp.concatenate(quarters, axis=1))
        return jnp.concatenate(rows, axis=0).reshape(TOKENS, width)

    last_ra = (lax.axis_index("ra") == lax.axis_size("ra") - 1).astype(jnp.int32)
    last_dec = (lax.axis_index("dec") == lax.axis_size("dec") - 1).astype(jnp.int32)
    last_freq = (lax.axis_index("freq") == lax.axis_size("freq") - 1).astype(jnp.int32)
    lane = lax.broadcasted_iota(jnp.int32, (1, 128), 1) - (width - 128)

    weights = (
        ag_ref[layer : layer + 1],
        qkv_s,
        out_ref,
        mg_ref[layer : layer + 1],
        up_ref,
        down_s,
    )
    masks = []
    for i, j in windows:
        on_dec = last_dec if i == n_dec - 1 else 0
        on_freq = last_freq if j == n_freq - 1 else 0
        on = jnp.where(lane < 2, last_ra, jnp.where(lane < 4, on_dec, on_freq))
        masks.append((query_cols, key_cols, on.astype(f32)))

    own = []
    if merge:
        z = next(take)
        n_earlier, layout = merge
        n_line, n_col = z.shape[3] // HALF, z.shape[4]

        def put(out, i, j):
            out = out.astype(f32).reshape(WIN, HALF, 2, WIN, width)
            for v in range(2):
                for lanes, low in ((slice(128), 0), (slice(width - 128), 128)):
                    kept = out[:, :, v, :, low : low + 128]
                    place = (low // 128, v, slice(None), slice(i * HALF, i * HALF + HALF))
                    z[(*place, (j + 1) % n_col, slice(HALF), lanes)] = kept[:, :, :HALF]
                    z[(*place, j, slice(HALF, WIN), lanes)] = kept[:, :, HALF:]

        for source, n, i, j in layout:
            if source == n_earlier:
                own.append((n, i, j))
            else:
                put(earlier[source][n], i, j)

    def load():
        return [assemble(i, j) for i, j in windows]

    def store(outs):
        if keeps:
            for n, out in enumerate(outs):
                y_ref[n] = out
        for n, i, j in own:
            put(outs[n], i, j)

    run_blocks(load, masks, weights, safe_refs, store)
    if not merge:
        return

    lines = 2 * WIN * n_line * HALF * n_col * WIN
    flat = z.reshape(2 * lines, 128)
    groups = []
    for w in range(2):
        low = flat[pl.ds(w, lines // 2, stride=2), :]
        high = flat[pl.ds(lines + w, lines // 2, stride=2), :]
        picked = jnp.concatenate([low, high[:, : width - 128]], axis=1)
        groups.append(picked.reshape(2, HALF, 2, n_line * HALF * n_col * HALF, width))
    merge_in = [
        groups[w][v, :, u].reshape(-1, width) for u in range(2) for v in range(2) for w in range(2)
    ]
    total = merge_in[0]
    for value in merge_in[1:]:
        total = total + value
    mean = jnp.sum(total, axis=-1, keepdims=True) * f32(1 / (8 * width))
    centred = [value - mean for value in merge_in]
    total = centred[0] * centred[0]
    for value in centred[1:]:
        total = total + value * value
    scale = lax.rsqrt(jnp.sum(total, axis=-1, keepdims=True) * f32(1 / (8 * width)) + 1e-05)
    merged = None
    for n, value in enumerate(centred):
        normed = (value * scale * gain_ref[:, n * width : (n + 1) * width]).astype(bf16)
        term = dot_f32(normed, merge_ref[n * width : (n + 1) * width])
        merged = term if merged is None else merged + term
    if n_col == 1:
        for n in range(merged.shape[0] // HALF):
            place = (n // (n_line * HALF), n % (n_line * HALF))
            g_ref[place] = merged[n * HALF : n * HALF + HALF // 2].astype(bf16)
    else:
        g_ref[...] = merged.astype(bf16).reshape(g_ref.shape)


def second_block(windows, n_freq, n_dec, pieces, args, merge=None, keeps=True, extra=()):
    width = args[1].shape[1]
    inputs, places = [], {}
    for key in pieces_of(windows, n_freq):
        places[key] = []
        for array, *place in pieces[key]:
            known = [n for n, other in enumerate(inputs) if other is array]
            if not known:
                known = [len(inputs)]
                inputs.append(array)
            places[key].append((known[0], *place))
    n_arrays = len(inputs)
    specs = [whole_spec(p.shape) for p in inputs] + weight_specs(1, args, 1)
    inputs += args
    scratch = weight_scratch(args)
    shapes = [(len(windows), TOKENS, width)] if keeps else []
    plan = None
    if merge is not None:
        gain, merge_weight, earlier, layout, (n_line, n_col) = merge
        more = [*earlier, gain.reshape(1, 8 * width), merge_weight]
        inputs += more
        specs += [whole_spec(m.shape) for m in more]
        plan = (len(earlier), layout)
        freq = HALF // 2 if n_col == 1 else n_col * HALF
        shapes.append((HALF, n_line * HALF, freq, merge_weight.shape[1]))
        scratch.append(pltpu.VMEM((2, 2, WIN, n_line * HALF, n_col, WIN, 128), f32))
    inputs += extra
    specs += [pl.BlockSpec(memory_space=pl.ANY) for _ in extra]
    return pl.pallas_call(
        functools.partial(
            second_kernel, 1, windows, n_freq, n_dec, places, n_arrays, plan, keeps, len(extra)
        ),
        grid=(1,),
        in_specs=specs,
        out_specs=[whole_spec(shape) for shape in shapes],
        out_shape=[jax.ShapeDtypeStruct(shape, bf16) for shape in shapes],
        scratch_shapes=scratch,
        compiler_params=pltpu.CompilerParams(vmem_limit_bytes=VMEM_LIMIT),
        cost_estimate=cost(len(windows), width, args),
    )(*inputs)


def send(value, steps):
    axes = tuple(steps)
    sizes = [lax.axis_size(axis) for axis in axes]
    total = 1
    for size in sizes:
        total *= size
    pairs = []
    for source in range(total):
        rest, coords = source, []
        for size in reversed(sizes):
            coords.insert(0, rest % size)
            rest //= size
        target = 0
        for axis, size, coord in zip(axes, sizes, coords):
            target = target * size + (coord - steps[axis]) % size
        pairs.append((source, target))
    return lax.ppermute(value, axes, pairs)


def on_device(
    tokens,
    attn_gain,
    qkv_weight,
    out_weight,
    mlp_gain,
    up_weight,
    down_weight,
    merge_gain,
    merge_weight,
):
    args = (
        attn_gain,
        qkv_weight,
        out_weight,
        mlp_gain,
        up_weight,
        jnp.swapaxes(down_weight, 1, 2),
    )
    n_dec, n_freq = tokens.shape[1] // WIN, tokens.shape[2] // WIN
    to_ra, to_dec, to_freq = {"ra": 1}, {"dec": 1}, {"freq": 1}
    pieces = {}
    ends, ahead = [None] * n_dec, None
    for pair in range(n_freq // 2):
        last = pair == n_freq // 2 - 1
        together = None
        for row in range(n_dec):
            limit = FIRST_LIMIT if pair == row == 0 else VMEM_LIMIT
            late, early, *rest = first_block(
                tokens,
                args,
                pair,
                row,
                ends[row] if last else None,
                ahead if last and row == 0 else None,
                together if not last and row > 0 else None,
                limit,
            )
            pieces[pair, row] = [(late, 0, 0, late.shape[1])]
            if row == 0:
                dec_part, *rest = rest
                ahead_now = send(dec_part, to_dec)
                pieces[pair, n_dec] = [(ahead_now, HALF, 0, ahead_now.shape[1])]
            if not last:
                ends[row] = send(rest[0], to_freq)
                together = early
                continue
            if row == n_dec - 1:
                early = jnp.concatenate([early, ahead_now[:HALF]], axis=1)
            moved = send(early, to_ra)
            rows = late.shape[1]
            pieces[pair, row].append((moved, 0, 0, rows))
            if row == 0 and ahead is not None:
                pieces[pair - 1, n_dec].append((moved, 0, rows, HALF))
            if row == n_dec - 1:
                pieces[pair, n_dec].append((moved, 0, rows, ahead_now.shape[1]))
        if not last:
            moved = send(together, to_ra)
            for row in range(n_dec):
                pieces[pair, row].append((moved, 0, row * WIN, WIN))
            ahead = ahead_now

    end = n_freq - 1
    (column_0,) = second_block([(0, 0), (1, 0)], n_freq, n_dec, pieces, args)
    column_end, edge = second_block(
        [(0, end), (1, end)],
        n_freq,
        n_dec,
        pieces,
        args,
        (merge_gain, merge_weight, [], [(0, 0, 0, 0), (0, 1, 1, 0)], (2, 1)),
    )
    edge = send(edge, {"freq": -1})

    def middle(i, extra):
        windows = [(i, j) for j in range(1, end)]
        layout = [(0, i, 0, 0), (1, i, 0, end)] + [(2, j - 1, 0, j) for j in range(1, end)]
        merge = (merge_gain, merge_weight, [column_0, column_end], layout, (1, n_freq))
        return second_block(windows, n_freq, n_dec, pieces, args, merge, False, extra)[0]

    q = HALF // 2
    high = middle(1, [])
    high = jnp.concatenate([edge[:, HALF:], high[:, :, q:]], axis=2)
    incoming = send(high[:, -q:], {"dec": -1})
    low = middle(0, [high])
    low = jnp.concatenate([edge[:, :HALF], low[:, :, q:]], axis=2)
    grid = jnp.concatenate([incoming, low, high[:, :-q]], axis=1)
    incoming = send(grid[-q:], {"ra": -1})
    return jnp.concatenate([incoming, grid[:-q]], axis=0)


def solution(mesh):
    placed = (P("ra", "dec", "freq", None), P(), P(), P(), P(), P(), P(), P(), P())
    return jax.shard_map(
        on_device,
        mesh=mesh,
        in_specs=placed,
        out_specs=P("ra", "dec", "freq", None),
        check_vma=False,
    )
```
